32 devices in a mesh: slab: 2 (over x), plane: 8 (over z, y), brick: 2 (over core).
Axes of the slice: x: 2, y: 2, z: 4, core: 2. Of those that a mesh axis runs over, the one named last changes fastest.
Arguments:
- camera_rows: bfloat16 [4, 16, 32, 2048], P(None, 'slab', ('plane', 'brick')), parts along dimension 1, may hold values from 0.19921875 to 5
- estimate: float32 [16, 32, 2048], P('slab', None, ('plane', 'brick')), parts along dimension 0, may hold values from 0.2 to 5
- psf_bank: float32 [32, 4, 3, 31], P(('slab', 'plane', 'brick')), parts along dimension 0, may hold values from 0 to 1.25, as said below
- psf_owner: int32 [32], P('slab'), parts along dimension 0, may hold values from 0 to 15, each once
- view_mask: int32 [32, 4], P('slab'), parts along dimension 0, may hold values 0 or 1
Outputs:
- deconvolved: float32 [16, 32, 2048], P('slab', None, ('plane', 'brick')), parts along dimension 0
The draws below stay inside these ranges and needn't reach their ends.
There are 2 independent parts, one for each index of `slab`. The reference program is written for one: setup_inputs(seed, part) draws one part's arguments, and reference() takes and returns one part's arrays. A program takes and returns all parts, laid end to end along the dimension named above; each array names one. Nothing has to cross between parts.
Inputs may be any that keep to these rules, and one draw needn't show every extreme that they name: `psf_owner`: every brick names a different device: the map is a permutation of 0 to 15. `psf_bank`: every tap is positive.
All inputs are finite; a program needn't handle non-finite values.
Results may differ from the reference program's by a relative error of at most 0.0003.
Values may be sent and summed in bfloat16 or wider, within the bound.
A program may use at most 192 MiB of HBM per device.

```python
import math
import jax
import jax.numpy as jnp
from jax import lax

V = 4
RADIUS = 15
TAPS = 31
ZD = 8
ITERS = 2
BRICKS = 16
ROWS = 32
COLS = 2048


def draw_psf_bank(key, part):
    key_width = jax.random.fold_in(key, 11)
    key_jitter = jax.random.fold_in(key, 23)
    low_end = jnp.array([5.0, 3.0, 3.0], jnp.float32)[:, None]
    high_end = jnp.array([9.0, 6.0, 6.0], jnp.float32)[:, None]
    fraction = jax.random.uniform(key_width, (BRICKS, V, 3, 1), jnp.float32)
    spread_width = low_end + fraction * (high_end - low_end)
    jitter_range = 0.2
    offsets = jnp.arange(TAPS, dtype=jnp.float32) - RADIUS
    profile = jnp.exp(-0.5 * (offsets / spread_width) ** 2)
    jitter_factor = jnp.exp(jax.random.uniform(key_jitter, (BRICKS, V, 3, TAPS), jnp.float32, minval=-jitter_range, maxval=jitter_range))
    return (profile * jitter_factor).astype(jnp.float32)


def touch_ends(values, stream_key, smallest, top_value):
    shape = values.shape
    spot = [jax.random.randint(jax.random.fold_in(stream_key, axis), (), 0, shape[axis]) for axis in range(len(shape))]
    values = values.at[tuple(spot)].set(smallest)
    longest = shape.index(max(shape))
    spot[longest] = (spot[longest] + 1) % shape[longest]
    return values.at[tuple(spot)].set(top_value)


def block_scale(rng, extent, cuts, low, largest):
    factor_of = 1.0
    for position, parts in cuts:
        draws = jax.random.uniform(jax.random.fold_in(jax.random.fold_in(rng, 6), position), (parts,), jnp.float32, low / len(cuts), largest / len(cuts))
        factor_of = factor_of * jnp.repeat(jnp.exp(draws), extent[position] // parts).reshape((-1,) + (1,) * (len(extent) - 1 - position))
    return factor_of


def setup_inputs(seed: int = 0, part: int = 0) -> dict:
    arg_keys = jax.random.split(jax.random.key(seed), 6)
    part_splits = jax.random.split(jax.random.fold_in(arg_keys[5], part), 6)
    return {
        "camera_rows": jnp.clip(jnp.exp(math.log(5.0) - 3.2227897 * jax.random.uniform(part_splits[0], (V, ZD, ROWS, COLS), jnp.float32) ** block_scale(part_splits[0], (V, ZD, ROWS, COLS), ((2, 16),), -0.2, 0.2)), 0.19921875, 5.0).astype(jnp.bfloat16),
        "estimate": jnp.clip(jnp.exp(math.log(5.0) - 3.218876 * jax.random.uniform(part_splits[1], (ZD, ROWS, COLS), jnp.float32) ** block_scale(part_splits[1], (ZD, ROWS, COLS), ((2, 16),), -0.2, 0.2)), 0.2, 5.0),
        "psf_bank": draw_psf_bank(jax.random.fold_in(jax.random.fold_in(arg_keys[5], part), 71), part),
        "psf_owner": jax.random.permutation(part_splits[3], BRICKS).astype(jnp.int32),
        "view_mask": touch_ends((jax.random.randint(part_splits[4], (BRICKS, V), 0, 4) < 3).astype(jnp.int32), jax.random.fold_in(part_splits[4], 1), 0, 1),
    }


BACKGROUND = 0.1
HIGHEST = lax.Precision.HIGHEST


def banded(profiles, size_in, size_out, offset):
    tap_count = profiles.shape[-1]
    centre = tap_count // 2
    lag_index = (jnp.arange(size_in, dtype=jnp.int32)[:, None]
                 - jnp.arange(size_out, dtype=jnp.int32)[None, :] - offset + centre)
    one_hot = (lag_index[:, :, None] == jnp.arange(tap_count, dtype=jnp.int32)[None, None, :]).astype(jnp.float32)
    return jnp.einsum("ijt,vt->vij", one_hot, profiles, precision=HIGHEST)


def convolve(volume, profiles, brick_width):
    depth_count = volume.shape[-3]
    row_count = volume.shape[-2]
    band_x = banded(profiles[:, 2], brick_width + 2 * RADIUS, brick_width, RADIUS)
    band_y = banded(profiles[:, 1], row_count, row_count, 0)
    band_z = banded(profiles[:, 0], depth_count, depth_count, 0)
    if volume.ndim == 3:
        section_one = jnp.einsum("zyi,vij->vzyj", volume, band_x, precision=HIGHEST)
    else:
        section_one = jnp.einsum("vzyi,vij->vzyj", volume, band_x, precision=HIGHEST)
    section_two = jnp.einsum("vziw,vij->vzjw", section_one, band_y, precision=HIGHEST)
    return jnp.einsum("vzyw,vzu->vuyw", section_two, band_z, precision=HIGHEST)


def reference(camera_rows, estimate, psf_bank, psf_owner, view_mask):
    view_count, depth_count, row_count, col_count = camera_rows.shape
    brick_width = col_count // BRICKS
    kernels = psf_bank[psf_owner]
    kernels = kernels / jnp.sum(kernels, axis=-1, keepdims=True)
    brick_ids = jnp.arange(BRICKS, dtype=jnp.int32)
    current = estimate
    for iteration in range(ITERS):
        padded = jnp.pad(current, ((0, 0), (0, 0), (RADIUS, RADIUS)))

        def ratio_of(brick_id):
            first_col = brick_id * brick_width
            window = lax.dynamic_slice_in_dim(padded, first_col, brick_width + 2 * RADIUS, 2)
            blurred = convolve(window, kernels[brick_id], brick_width)
            data_piece = lax.dynamic_slice_in_dim(camera_rows, first_col, brick_width, 3).astype(jnp.float32)
            seen_views = view_mask[brick_id] > 0
            return jnp.where(seen_views[:, None, None, None], data_piece / (blurred + BACKGROUND), 0.0)

        ratios = lax.map(ratio_of, brick_ids)
        quotient = jnp.transpose(ratios, (1, 2, 3, 0, 4)).reshape(view_count, depth_count, row_count, col_count)
        quotient_pad = jnp.pad(quotient, ((0, 0), (0, 0), (0, 0), (RADIUS, RADIUS)))

        def update_of(brick_id):
            first_col = brick_id * brick_width
            window = lax.dynamic_slice_in_dim(quotient_pad, first_col, brick_width + 2 * RADIUS, 3)
            corrected = convolve(window, kernels[brick_id][:, :, ::-1], brick_width)
            seen_views = view_mask[brick_id] > 0
            factor = jnp.sum(jnp.where(seen_views[:, None, None, None], corrected, 1.0), axis=0) / view_count
            return lax.dynamic_slice_in_dim(current, first_col, brick_width, 2) * factor

        pieces = lax.map(update_of, brick_ids)
        current = jnp.transpose(pieces, (1, 2, 0, 3)).reshape(depth_count, row_count, col_count)
    return current
```

```python
import functools

import jax
import jax.numpy as jnp
from jax import lax
from jax.experimental import pallas as pl
from jax.experimental.pallas import tpu as pltpu
from jax.sharding import PartitionSpec as P

V = 4
RADIUS = 15
ITERS = 2
EDGE = 16


BACKGROUND = 0.1
HIGHEST = lax.Precision.HIGHEST
F32 = jnp.float32
BF16 = jnp.bfloat16
def padded_2(cells, sides, width):
    for axis, dim in sides:
        count = lax.axis_size(axis)
        ends = count - 1
        head = lax.slice_in_dim(cells, 0, width, axis=dim)
        tail = lax.slice_in_dim(cells, cells.shape[dim] - width, cells.shape[dim], axis=dim)
        cells = jnp.concatenate(
            [
                lax.ppermute(tail, axis, [(i, (i + 1) % count) for i in range(ends)]),
                cells,
                lax.ppermute(head, axis, [((i + 1) % count, i) for i in range(ends)]),
            ],
            axis=dim,
        )
    return cells


def banded(profiles, size_in, size_out, offset):
    tap_count = profiles.shape[-1]
    centre = tap_count // 2
    lag_index = (
        jnp.arange(size_in, dtype=jnp.int32)[:, None]
        - jnp.arange(size_out, dtype=jnp.int32)[None, :]
        - offset
        + centre
    )
    one_hot = (
        lag_index[:, :, None] == jnp.arange(tap_count, dtype=jnp.int32)[None, None, :]
    ).astype(jnp.float32)
    return jnp.einsum("ijt,vt->vij", one_hot, profiles, precision=HIGHEST)


def across_columns(volume, band_x):
    if volume.ndim == 3:
        return jnp.einsum("zyi,vij->vzyj", volume, band_x, precision=HIGHEST)
    return jnp.einsum("vzyi,vij->vzyj", volume, band_x, precision=HIGHEST)


def across_rows(volume, band_y):
    view_count, depth_count, row_count, col_count = volume.shape
    block_rows = band_y.shape[2]
    margin = (band_y.shape[1] - block_rows) // 2
    pieces = volume.reshape(view_count, depth_count, row_count // block_rows, block_rows, col_count)
    blanks = jnp.zeros((view_count, depth_count, 1, margin, col_count), jnp.float32)
    before = jnp.concatenate([blanks, pieces[:, :, :-1, block_rows - margin :, :]], axis=2)
    behind = jnp.concatenate([pieces[:, :, 1:, :margin, :], blanks], axis=2)
    windows = jnp.concatenate([before, pieces, behind], axis=3)
    result = jnp.einsum("vzqic,vij->vzqjc", windows, band_y, precision=HIGHEST)
    return result.reshape(view_count, depth_count, row_count, col_count)


def across_depth(volume, band_z):
    return jnp.einsum("vzyc,vzw->vwyc", volume, band_z, precision=HIGHEST)


def separable(volume, bands):
    return across_depth(across_rows(across_columns(volume, bands[0]), bands[1]), bands[2])


def shards(camera_rows, estimate, psf_bank, psf_owner, view_mask):
    regrouped = lax.all_to_all(
        camera_rows, ("plane", "brick"), split_axis=3, concat_axis=2, tiled=True
    )
    position = lax.axis_index(("plane", "brick"))
    brick_ids = jnp.arange(psf_owner.shape[0], dtype=jnp.int32)
    is_mine = brick_ids == position
    owner_id = jnp.sum(jnp.where(is_mine, psf_owner, 0))
    observed = jnp.sum(jnp.where(is_mine[:, None], view_mask, 0), axis=0) > 0
    fitted = lax.all_gather(psf_bank, ("plane", "brick"), axis=0, tiled=True)
    chosen = (brick_ids == owner_id).astype(jnp.float32)
    kernels = jnp.einsum("b,bvat->vat", chosen, fitted, precision=HIGHEST)
    kernels = kernels / jnp.sum(kernels, axis=-1, keepdims=True)
    flipped = kernels[:, :, ::-1]
    depth_size = estimate.shape[0]
    row_size = estimate.shape[1]
    col_size = estimate.shape[2]
    block_size = 128 if row_size % 128 == 0 else row_size

    def make_bands(profiles):
        return (
            banded(profiles[:, 2], col_size + 2 * RADIUS, col_size, RADIUS),
            banded(profiles[:, 1], block_size + 2 * RADIUS, block_size, RADIUS),
            banded(profiles[:, 0], depth_size, depth_size, 0),
        )

    blur_bands = make_bands(kernels)
    back_bands = make_bands(flipped)
    current = estimate
    for iteration in range(ITERS):
        padded = padded_2(current.astype(jnp.bfloat16), ((("plane", "brick"), 2),), RADIUS).astype(
            current.dtype
        )
        blurred = separable(padded, blur_bands)
        quotient = jnp.where(
            observed[:, None, None, None],
            regrouped.astype(jnp.float32) / (blurred + BACKGROUND),
            0.0,
        )
        quotient_wide = padded_2(
            quotient.astype(jnp.bfloat16), ((("plane", "brick"), 3),), RADIUS
        ).astype(quotient.dtype)
        corrected = separable(quotient_wide, back_bands)
        factor = jnp.sum(jnp.where(observed[:, None, None, None], corrected, 1.0), axis=0) / V
        current = current * factor
    return current


def split(a):
    hi = a.astype(BF16)
    return hi, (a - hi.astype(F32)).astype(BF16)


def dot(a, b, nt=False):
    dims = (((1,), (1 if nt else 0,)), ((), ()))
    return lax.dot_general(a, b, dims, preferred_element_type=F32)


def dot3(a, b, nt=False):
    return dot(a[0], b[0], nt) + (dot(a[0], b[1], nt) + dot(a[1], b[0], nt))


def dot2(a, b, nt=False):
    return dot(a, b[0], nt) + dot(a, b[1], nt)


def exact(a, b):
    return lax.dot_general(a, b, (((1,), (0,)), ((), ())), precision=HIGHEST, preferred_element_type=F32)


def fused(
    dims, cam, est, psf, owner, mask, out,
    taps, gath, camrecv, camt, xsend, xhalo, rsend, rhalo, kbh, kbl, abl, aback, xt,
    psf_sems, cam_sems, x_sems, r_sems, own_sem,
):
    n, brick, zd, rows, cols = dims
    lr = rows // n
    part = zd * lr
    cells = zd * rows
    taps_n = psf.shape[-1]
    me = lax.axis_index("plane") * brick + lax.axis_index("brick")

    def device(t):
        return {"plane": lax.div(t, brick), "brick": lax.rem(t, brick)}

    def peer(k):
        return lax.rem(me + k, n)

    barrier = pltpu.get_barrier_semaphore()
    for k in range(1, n):
        pl.semaphore_signal(barrier, inc=1, device_id=device(peer(k)), device_id_type=pl.DeviceIdType.MESH)

    has_left = me > 0
    has_right = me < n - 1
    zero_edge = jnp.zeros((EDGE, cells), BF16)

    @pl.when(me == 0)
    def _():
        for it in range(ITERS):
            xhalo[it, 0:EDGE, :] = zero_edge
            for v in range(V):
                rhalo[it, v, 0:EDGE, :] = zero_edge

    @pl.when(me == n - 1)
    def _():
        for it in range(ITERS):
            xhalo[it, EDGE:, :] = zero_edge
            for v in range(V):
                rhalo[it, v, EDGE:, :] = zero_edge

    def x_copy(it, side):
        rows_of = pl.ds(side * EDGE, EDGE)
        return pltpu.make_async_remote_copy(
            src_ref=xsend.at[it, rows_of], dst_ref=xhalo.at[it, rows_of],
            send_sem=x_sems.at[0, it, side], recv_sem=x_sems.at[1, it, side],
            device_id=device(lax.rem(me + n + 1 - 2 * side, n)), device_id_type=pl.DeviceIdType.MESH,
        )

    def r_copy(it, side):
        rows_of = pl.ds(side * EDGE, EDGE)
        return pltpu.make_async_remote_copy(
            src_ref=rsend.at[it, :, rows_of], dst_ref=rhalo.at[it, :, rows_of],
            send_sem=r_sems.at[0, it, side], recv_sem=r_sems.at[1, it, side],
            device_id=device(lax.rem(me + n + 1 - 2 * side, n)), device_id_type=pl.DeviceIdType.MESH,
        )

    def start(make, it):
        @pl.when(has_right)
        def _():
            make(it, 0).start()

        @pl.when(has_left)
        def _():
            make(it, 1).start()

    def arrive(make, it):
        @pl.when(has_left)
        def _():
            make(it, 0).wait_recv()

        @pl.when(has_right)
        def _():
            make(it, 1).wait_recv()

    def finish(make, it):
        @pl.when(has_right)
        def _():
            make(it, 0).wait_send()

        @pl.when(has_left)
        def _():
            make(it, 1).wait_send()

    def psf_copy(k):
        return pltpu.make_async_remote_copy(
            src_ref=psf.at[0], dst_ref=gath.at[me],
            send_sem=psf_sems.at[0, k], recv_sem=psf_sems.at[1, k],
            device_id=device(peer(k)), device_id_type=pl.DeviceIdType.MESH,
        )

    def cam_copy(k):
        return pltpu.make_async_remote_copy(
            src_ref=cam.at[:, pl.ds(pl.multiple_of(peer(k) * cols, cols), cols)], dst_ref=camrecv.at[me],
            send_sem=cam_sems.at[0, k], recv_sem=cam_sems.at[1, k],
            device_id=device(peer(k)), device_id_type=pl.DeviceIdType.MESH,
        )

    own = pltpu.make_async_copy(
        cam.at[:, pl.ds(pl.multiple_of(me * cols, cols), cols)], camrecv.at[me], own_sem
    )
    own.start()
    x0 = est[...].T
    xt[...] = x0
    xsend[0, 0:EDGE, :] = x0[cols - EDGE :, :].astype(BF16)
    xsend[0, EDGE:, :] = x0[:EDGE, :].astype(BF16)
    gath[me] = psf[0]

    pl.semaphore_wait(barrier, n - 1)
    for k in range(1, n):
        psf_copy(k).start()
    start(x_copy, 0)
    for k in range(1, n):
        cam_copy(k).start()

    lane = lax.broadcasted_iota(jnp.int32, (128, cells), 1)
    line = lax.broadcasted_iota(jnp.int32, (128, cells), 0)
    y_of = lax.shift_right_logical(lane, part.bit_length() - 1) * lr + (lane & (lr - 1))
    z_of = lax.shift_right_logical(lane, lr.bit_length() - 1) & (zd - 1)
    pick_y = (y_of == line).astype(F32)
    pick_z = (z_of == line).astype(F32)
    flip = (
        lax.broadcasted_iota(jnp.int32, (128, 128), 0) + lax.broadcasted_iota(jnp.int32, (128, 128), 1)
        == taps_n - 1
    ).astype(F32)
    taps[...] = jnp.zeros_like(taps)

    for k in range(1, n):
        psf_copy(k).wait_recv()
    block = gath[owner[me]]
    for a in range(3):
        for v in range(V):
            taps[pl.ds(a * V + v, 1), 0:taps_n] = block[v, a : a + 1, :]
    kernels = taps[...]
    total = jnp.sum(kernels, axis=-1, keepdims=True)
    kernels = kernels / jnp.where(total > 0.0, total, 1.0)
    flipped = exact(kernels, flip)

    def toeplitz(row, height, width):
        if width > 128:
            row = jnp.concatenate([row, jnp.zeros((1, width - 128), F32)], axis=1)
        return pltpu.roll(
            jnp.broadcast_to(row, (height, width)), width - RADIUS, 1, stride=1, stride_axis=0
        )

    lines_y = jnp.concatenate([toeplitz(flipped[V + v : V + v + 1], rows, 128) for v in range(V)], axis=0)
    lines_z = jnp.concatenate([toeplitz(flipped[v : v + 1], zd, 128) for v in range(V)], axis=0)
    wide_y = exact(lines_y, pick_y)
    wide_z = exact(lines_z, pick_z)
    seen = [mask[me, v] > 0 for v in range(V)]
    back_edge = jnp.zeros((cols, 128), F32)
    for v in range(V):
        for z in range(zd):
            piece = wide_y[v * rows : (v + 1) * rows] * wide_z[v * zd + z : v * zd + z + 1]
            hi, lo = split(piece)
            kbh[v, z * rows : (z + 1) * rows, :] = hi
            kbl[v, z * rows : (z + 1) * rows, :] = lo
        band = toeplitz(kernels[2 * V + v : 2 * V + v + 1], cols, 2 * cols)
        hi, lo = split(band[:, :cols])
        abl[0, v] = hi
        abl[1, v] = lo
        hi, lo = split(pltpu.roll(band[:, cols:], EDGE, 1))
        abl[2, v] = hi
        abl[3, v] = lo
        band = jnp.where(seen[v], toeplitz(flipped[2 * V + v : 2 * V + v + 1], cols, 2 * cols), 0.0)
        hi, lo = split(band[:, :cols])
        aback[0, v] = hi
        aback[1, v] = lo
        back_edge = back_edge + pltpu.roll(band[:, cols:], (EDGE + 2 * EDGE * v) % 128, 1)
    back_edge = split(back_edge)
    unseen = functools.reduce(jnp.add, [jnp.where(s, 0.0, 1.0) for s in seen])

    for it in range(ITERS):
        x = split(xt[...])
        blurred = []
        for v in range(V):
            spread = split(dot3(x, (kbh[v], kbl[v])))
            blurred.append(dot3((abl[0, v], abl[1, v]), spread))
        arrive(x_copy, it)
        edge = xhalo[it]
        for v in range(V):
            spread = split(dot2(edge, (kbh[v], kbl[v])))
            blurred[v] = blurred[v] + dot3((abl[2, v, :, 0 : 2 * EDGE], abl[3, v, :, 0 : 2 * EDGE]), spread)
        if it == 0:
            for k in range(1, n):
                cam_copy(k).wait_recv()
            own.wait()
            for v in range(V):
                tile = camrecv[:, v * part : (v + 1) * part, :].reshape(cells, cols)
                camt[v] = tile.astype(F32).T
        ratios = []
        for v in range(V):
            ratio = jnp.where(seen[v], camt[v] / (blurred[v] + BACKGROUND), 0.0)
            rsend[it, v, 0:EDGE, :] = ratio[cols - EDGE :, :].astype(BF16)
            rsend[it, v, EDGE:, :] = ratio[:EDGE, :].astype(BF16)
            ratios.append(ratio)
        start(r_copy, it)
        total = jnp.zeros((cols, cells), F32)
        for v in range(V):
            spread = split(dot3(split(ratios[v]), (kbh[v], kbl[v]), nt=True))
            total = total + dot3((aback[0, v], aback[1, v]), spread)
        arrive(r_copy, it)
        spread = [dot2(rhalo[it, v], (kbh[v], kbl[v]), nt=True) for v in range(V)]
        total = total + dot3(back_edge, split(jnp.concatenate(spread, axis=0)))
        fresh = xt[...] * ((total + unseen) * (1.0 / V))
        if it < ITERS - 1:
            xsend[it + 1, 0:EDGE, :] = fresh[cols - EDGE :, :].astype(BF16)
            xsend[it + 1, EDGE:, :] = fresh[:EDGE, :].astype(BF16)
            start(x_copy, it + 1)
            xt[...] = fresh
        else:
            out[...] = fresh.T

    for k in range(1, n):
        psf_copy(k).wait_send()
        cam_copy(k).wait_send()
    for it in range(ITERS):
        finish(x_copy, it)
        finish(r_copy, it)


def power_of_two(a):
    return a & (a - 1) == 0


def fused_shards(dims, camera_rows, estimate, psf_bank, psf_owner, view_mask):
    n, brick, zd, rows, cols = dims
    lr = rows // n
    cells = zd * rows
    vmem = pl.BlockSpec(memory_space=pltpu.VMEM)
    smem = pl.BlockSpec(memory_space=pltpu.SMEM)
    result = pl.pallas_call(
        functools.partial(fused, dims),
        out_shape=jax.ShapeDtypeStruct((cells, cols), F32),
        in_specs=[vmem, vmem, vmem, smem, smem],
        out_specs=vmem,
        scratch_shapes=[
            pltpu.VMEM((16, 128), F32),
            pltpu.VMEM((n,) + psf_bank.shape[1:], F32),
            pltpu.VMEM((n, V * zd * lr, cols), BF16),
            pltpu.VMEM((V, cols, cells), F32),
            pltpu.VMEM((ITERS, 2 * EDGE, cells), BF16),
            pltpu.VMEM((ITERS, 2 * EDGE, cells), BF16),
            pltpu.VMEM((ITERS, V, 2 * EDGE, cells), BF16),
            pltpu.VMEM((ITERS, V, 2 * EDGE, cells), BF16),
            pltpu.VMEM((V, cells, cells), BF16),
            pltpu.VMEM((V, cells, cells), BF16),
            pltpu.VMEM((4, V, cols, cols), BF16),
            pltpu.VMEM((2, V, cols, cols), BF16),
            pltpu.VMEM((cols, cells), F32),
            pltpu.SemaphoreType.DMA((2, n)),
            pltpu.SemaphoreType.DMA((2, n)),
            pltpu.SemaphoreType.DMA((2, ITERS, 2)),
            pltpu.SemaphoreType.DMA((2, ITERS, 2)),
            pltpu.SemaphoreType.DMA,
        ],
        compiler_params=pltpu.CompilerParams(
            collective_id=0, has_side_effects=True, vmem_limit_bytes=32 * 1024 * 1024
        ),
    )(
        camera_rows.reshape(V * zd * lr, n * cols),
        estimate.reshape(cells, cols),
        psf_bank,
        psf_owner,
        view_mask,
    )
    return result.reshape(zd, rows, cols)


def solution(mesh):
    n = mesh.shape["plane"] * mesh.shape["brick"]

    def shards_of(camera_rows, estimate, psf_bank, psf_owner, view_mask):
        zd, rows, cols = estimate.shape
        lr = camera_rows.shape[2]
        small = (
            zd * rows == 256
            and cols == 128
            and psf_bank.shape[-1] == 2 * RADIUS + 1
            and lr * n == rows
            and zd % 8 == 0
            and zd * lr % 16 == 0
            and power_of_two(zd)
            and power_of_two(lr)
        )
        if not small:
            return shards(camera_rows, estimate, psf_bank, psf_owner, view_mask)
        dims = (n, mesh.shape["brick"], zd, rows, cols)
        return fused_shards(dims, camera_rows, estimate, psf_bank, psf_owner, view_mask)

    return jax.shard_map(
        shards_of,
        mesh=mesh,
        in_specs=(
            P(None, "slab", ("plane", "brick"), None),
            P("slab", None, ("plane", "brick")),
            P(("slab", "plane", "brick"), None, None, None),
            P("slab"),
            P("slab", None),
        ),
        out_specs=P("slab", None, ("plane", "brick")),
        check_vma=False,
    )
```

```python
import functools

import jax
import jax.numpy as jnp
from jax import lax
from jax.experimental import pallas as pl
from jax.experimental.pallas import tpu as pltpu
from jax.sharding import PartitionSpec as P

V = 4
RADIUS = 15
ITERS = 2
EDGE = 16


BACKGROUND = 0.1
HIGHEST = lax.Precision.HIGHEST
F32 = jnp.float32
BF16 = jnp.bfloat16
def padded_2(cells, sides, width):
    for axis, dim in sides:
        count = lax.axis_size(axis)
        ends = count - 1
        head = lax.slice_in_dim(cells, 0, width, axis=dim)
        tail = lax.slice_in_dim(cells, cells.shape[dim] - width, cells.shape[dim], axis=dim)
        cells = jnp.concatenate(
            [
                lax.ppermute(tail, axis, [(i, (i + 1) % count) for i in range(ends)]),
                cells,
                lax.ppermute(head, axis, [((i + 1) % count, i) for i in range(ends)]),
            ],
            axis=dim,
        )
    return cells


def banded(profiles, size_in, size_out, offset):
    tap_count = profiles.shape[-1]
    centre = tap_count // 2
    lag_index = (
        jnp.arange(size_in, dtype=jnp.int32)[:, None]
        - jnp.arange(size_out, dtype=jnp.int32)[None, :]
        - offset
        + centre
    )
    one_hot = (
        lag_index[:, :, None] == jnp.arange(tap_count, dtype=jnp.int32)[None, None, :]
    ).astype(jnp.float32)
    return jnp.einsum("ijt,vt->vij", one_hot, profiles, precision=HIGHEST)


def across_columns(volume, band_x):
    if volume.ndim == 3:
        return jnp.einsum("zyi,vij->vzyj", volume, band_x, precision=HIGHEST)
    return jnp.einsum("vzyi,vij->vzyj", volume, band_x, precision=HIGHEST)


def across_rows(volume, band_y):
    view_count, depth_count, row_count, col_count = volume.shape
    block_rows = band_y.shape[2]
    margin = (band_y.shape[1] - block_rows) // 2
    pieces = volume.reshape(view_count, depth_count, row_count // block_rows, block_rows, col_count)
    blanks = jnp.zeros((view_count, depth_count, 1, margin, col_count), jnp.float32)
    before = jnp.concatenate([blanks, pieces[:, :, :-1, block_rows - margin :, :]], axis=2)
    behind = jnp.concatenate([pieces[:, :, 1:, :margin, :], blanks], axis=2)
    windows = jnp.concatenate([before, pieces, behind], axis=3)
    result = jnp.einsum("vzqic,vij->vzqjc", windows, band_y, precision=HIGHEST)
    return result.reshape(view_count, depth_count, row_count, col_count)


def across_depth(volume, band_z):
    return jnp.einsum("vzyc,vzw->vwyc", volume, band_z, precision=HIGHEST)


def separable(volume, bands):
    return across_depth(across_rows(across_columns(volume, bands[0]), bands[1]), bands[2])


def shards(camera_rows, estimate, psf_bank, psf_owner, view_mask):
    regrouped = lax.all_to_all(
        camera_rows, ("plane", "brick"), split_axis=3, concat_axis=2, tiled=True
    )
    position = lax.axis_index(("plane", "brick"))
    brick_ids = jnp.arange(psf_owner.shape[0], dtype=jnp.int32)
    is_mine = brick_ids == position
    owner_id = jnp.sum(jnp.where(is_mine, psf_owner, 0))
    observed = jnp.sum(jnp.where(is_mine[:, None], view_mask, 0), axis=0) > 0
    fitted = lax.all_gather(psf_bank, ("plane", "brick"), axis=0, tiled=True)
    chosen = (brick_ids == owner_id).astype(jnp.float32)
    kernels = jnp.einsum("b,bvat->vat", chosen, fitted, precision=HIGHEST)
    kernels = kernels / jnp.sum(kernels, axis=-1, keepdims=True)
    flipped = kernels[:, :, ::-1]
    depth_size = estimate.shape[0]
    row_size = estimate.shape[1]
    col_size = estimate.shape[2]
    block_size = 128 if row_size % 128 == 0 else row_size

    def make_bands(profiles):
        return (
            banded(profiles[:, 2], col_size + 2 * RADIUS, col_size, RADIUS),
            banded(profiles[:, 1], block_size + 2 * RADIUS, block_size, RADIUS),
            banded(profiles[:, 0], depth_size, depth_size, 0),
        )

    blur_bands = make_bands(kernels)
    back_bands = make_bands(flipped)
    current = estimate
    for iteration in range(ITERS):
        padded = padded_2(current.astype(jnp.bfloat16), ((("plane", "brick"), 2),), RADIUS).astype(
            current.dtype
        )
        blurred = separable(padded, blur_bands)
        quotient = jnp.where(
            observed[:, None, None, None],
            regrouped.astype(jnp.float32) / (blurred + BACKGROUND),
            0.0,
        )
        quotient_wide = padded_2(
            quotient.astype(jnp.bfloat16), ((("plane", "brick"), 3),), RADIUS
        ).astype(quotient.dtype)
        corrected = separable(quotient_wide, back_bands)
        factor = jnp.sum(jnp.where(observed[:, None, None, None], corrected, 1.0), axis=0) / V
        current = current * factor
    return current


def split(a):
    hi = a.astype(BF16)
    return hi, (a - hi.astype(F32)).astype(BF16)


def dot(a, b, nt=False):
    dims = (((1,), (1 if nt else 0,)), ((), ()))
    return lax.dot_general(a, b, dims, preferred_element_type=F32)


def dot3(a, b, nt=False):
    return dot(a[0], b[0], nt) + (dot(a[0], b[1], nt) + dot(a[1], b[0], nt))


def dot2(a, b, nt=False):
    return dot(a, b[0], nt) + dot(a, b[1], nt)


def exact(a, b):
    return lax.dot_general(a, b, (((1,), (0,)), ((), ())), precision=HIGHEST, preferred_element_type=F32)


def fused(
    dims, cam, est, psf, owner, mask, out,
    taps, gath, camrecv, camt, xsend, xhalo, rsend, rhalo, kbh, kbl, abl, aback, xt,
    psf_sems, cam_sems, x_sems, r_sems, own_sem,
):
    n, brick, zd, rows, cols = dims
    lr = rows // n
    part = zd * lr
    cells = zd * rows
    taps_n = psf.shape[-1]
    me = lax.axis_index("plane") * brick + lax.axis_index("brick")

    def device(t):
        return {"plane": lax.div(t, brick), "brick": lax.rem(t, brick)}

    def peer(k):
        return lax.rem(me + k, n)

    barrier = pltpu.get_barrier_semaphore()
    for k in range(1, n):
        pl.semaphore_signal(barrier, inc=1, device_id=device(peer(k)), device_id_type=pl.DeviceIdType.MESH)

    has_left = me > 0
    has_right = me < n - 1
    zero_edge = jnp.zeros((EDGE, cells), BF16)

    @pl.when(me == 0)
    def _():
        for it in range(ITERS):
            xhalo[it, 0:EDGE, :] = zero_edge
            for v in range(V):
                rhalo[it, v, 0:EDGE, :] = zero_edge

    @pl.when(me == n - 1)
    def _():
        for it in range(ITERS):
            xhalo[it, EDGE:, :] = zero_edge
            for v in range(V):
                rhalo[it, v, EDGE:, :] = zero_edge

    def x_copy(it, side):
        rows_of = pl.ds(side * EDGE, EDGE)
        return pltpu.make_async_remote_copy(
            src_ref=xsend.at[it, rows_of], dst_ref=xhalo.at[it, rows_of],
            send_sem=x_sems.at[0, it, side], recv_sem=x_sems.at[1, it, side],
            device_id=device(lax.rem(me + n + 1 - 2 * side, n)), device_id_type=pl.DeviceIdType.MESH,
        )

    def r_copy(it, side):
        rows_of = pl.ds(side * EDGE, EDGE)
        return pltpu.make_async_remote_copy(
            src_ref=rsend.at[it, :, rows_of], dst_ref=rhalo.at[it, :, rows_of],
            send_sem=r_sems.at[0, it, side], recv_sem=r_sems.at[1, it, side],
            device_id=device(lax.rem(me + n + 1 - 2 * side, n)), device_id_type=pl.DeviceIdType.MESH,
        )

    def start(make, it):
        @pl.when(has_right)
        def _():
            make(it, 0).start()

        @pl.when(has_left)
        def _():
            make(it, 1).start()

    def arrive(make, it):
        @pl.when(has_left)
        def _():
            make(it, 0).wait_recv()

        @pl.when(has_right)
        def _():
            make(it, 1).wait_recv()

    def finish(make, it):
        @pl.when(has_right)
        def _():
            make(it, 0).wait_send()

        @pl.when(has_left)
        def _():
            make(it, 1).wait_send()

    def psf_copy(k):
        return pltpu.make_async_remote_copy(
            src_ref=psf.at[0], dst_ref=gath.at[me],
            send_sem=psf_sems.at[0, k], recv_sem=psf_sems.at[1, k],
            device_id=device(peer(k)), device_id_type=pl.DeviceIdType.MESH,
        )

    def cam_copy(k):
        return pltpu.make_async_remote_copy(
            src_ref=cam.at[:, pl.ds(pl.multiple_of(peer(k) * cols, cols), cols)], dst_ref=camrecv.at[me],
            send_sem=cam_sems.at[0, k], recv_sem=cam_sems.at[1, k],
            device_id=device(peer(k)), device_id_type=pl.DeviceIdType.MESH,
        )

    own = pltpu.make_async_copy(
        cam.at[:, pl.ds(pl.multiple_of(me * cols, cols), cols)], camrecv.at[me], own_sem
    )
    own.start()
    x0 = est[...].T
    xt[...] = x0
    xsend[0, 0:EDGE, :] = x0[cols - EDGE :, :].astype(BF16)
    xsend[0, EDGE:, :] = x0[:EDGE, :].astype(BF16)
    gath[me] = psf[0]

    pl.semaphore_wait(barrier, n - 1)
    far_first = sorted(range(1, n), key=lambda k: -min(k, n - k))
    for k in far_first:
        psf_copy(k).start()
    start(x_copy, 0)
    for k in far_first:
        cam_copy(k).start()

    lane = lax.broadcasted_iota(jnp.int32, (128, cells), 1)
    line = lax.broadcasted_iota(jnp.int32, (128, cells), 0)
    y_of = lax.shift_right_logical(lane, part.bit_length() - 1) * lr + (lane & (lr - 1))
    z_of = lax.shift_right_logical(lane, lr.bit_length() - 1) & (zd - 1)
    pick_y = (y_of == line).astype(F32)
    pick_z = (z_of == line).astype(F32)
    flip = (
        lax.broadcasted_iota(jnp.int32, (128, 128), 0) + lax.broadcasted_iota(jnp.int32, (128, 128), 1)
        == taps_n - 1
    ).astype(F32)
    taps[...] = jnp.zeros_like(taps)

    for k in range(1, n):
        psf_copy(k).wait_recv()
    block = gath[owner[me]]
    for a in range(3):
        taps[a * V : (a + 1) * V, 0:taps_n] = block[a]
    kernels = taps[...]
    total = jnp.sum(kernels, axis=-1, keepdims=True)
    kernels = kernels / jnp.where(total > 0.0, total, 1.0)
    flipped = exact(kernels, flip)

    def toeplitz(row, height, width):
        if width > 128:
            row = jnp.concatenate([row, jnp.zeros((1, width - 128), F32)], axis=1)
        return pltpu.roll(
            jnp.broadcast_to(row, (height, width)), width - RADIUS, 1, stride=1, stride_axis=0
        )

    lines_y = jnp.concatenate([toeplitz(flipped[V + v : V + v + 1], rows, 128) for v in range(V)], axis=0)
    lines_z = jnp.concatenate([toeplitz(flipped[v : v + 1], zd, 128) for v in range(V)], axis=0)
    wide_y = exact(lines_y, pick_y)
    wide_z = exact(lines_z, pick_z)
    seen = [mask[v, me] > 0 for v in range(V)]
    back_edge = jnp.zeros((cols, 128), F32)
    for v in range(V):
        for z in range(zd):
            piece = wide_y[v * rows : (v + 1) * rows] * wide_z[v * zd + z : v * zd + z + 1]
            hi, lo = split(piece)
            kbh[v, z * rows : (z + 1) * rows, :] = hi
            kbl[v, z * rows : (z + 1) * rows, :] = lo
        band = toeplitz(kernels[2 * V + v : 2 * V + v + 1], cols, 2 * cols)
        hi, lo = split(band[:, :cols])
        abl[0, v] = hi
        abl[1, v] = lo
        hi, lo = split(pltpu.roll(band[:, cols:], EDGE, 1))
        abl[2, v] = hi
        abl[3, v] = lo
        band = jnp.where(seen[v], toeplitz(flipped[2 * V + v : 2 * V + v + 1], cols, 2 * cols), 0.0)
        hi, lo = split(band[:, :cols])
        aback[0, v] = hi
        aback[1, v] = lo
        back_edge = back_edge + pltpu.roll(band[:, cols:], (EDGE + 2 * EDGE * v) % 128, 1)
    back_edge = split(back_edge)
    unseen = functools.reduce(jnp.add, [jnp.where(s, 0.0, 1.0) for s in seen])

    for it in range(ITERS):
        x = split(xt[...])
        blurred = []
        for v in range(V):
            spread = split(dot3(x, (kbh[v], kbl[v])))
            blurred.append(dot3((abl[0, v], abl[1, v]), spread))
        arrive(x_copy, it)
        edge = xhalo[it]
        for v in range(V):
            spread = split(dot2(edge, (kbh[v], kbl[v])))
            blurred[v] = blurred[v] + dot3((abl[2, v, :, 0 : 2 * EDGE], abl[3, v, :, 0 : 2 * EDGE]), spread)
        if it == 0:
            for k in range(1, n):
                cam_copy(k).wait_recv()
            own.wait()
            for v in range(V):
                tile = camrecv[:, v * part : (v + 1) * part, :].reshape(cells, cols)
                camt[v] = tile.astype(F32).T
        ratios = []
        for v in range(V):
            ratio = jnp.where(seen[v], camt[v] / (blurred[v] + BACKGROUND), 0.0)
            rsend[it, v, 0:EDGE, :] = ratio[cols - EDGE :, :].astype(BF16)
            rsend[it, v, EDGE:, :] = ratio[:EDGE, :].astype(BF16)
            ratios.append(ratio)
        start(r_copy, it)
        total = jnp.zeros((cols, cells), F32)
        for v in range(V):
            spread = split(dot3(split(ratios[v]), (kbh[v], kbl[v]), nt=True))
            total = total + dot3((aback[0, v], aback[1, v]), spread)
        arrive(r_copy, it)
        spread = [dot2(rhalo[it, v], (kbh[v], kbl[v]), nt=True) for v in range(V)]
        total = total + dot3(back_edge, split(jnp.concatenate(spread, axis=0)))
        fresh = xt[...] * ((total + unseen) * (1.0 / V))
        if it < ITERS - 1:
            xsend[it + 1, 0:EDGE, :] = fresh[cols - EDGE :, :].astype(BF16)
            xsend[it + 1, EDGE:, :] = fresh[:EDGE, :].astype(BF16)
            start(x_copy, it + 1)
            xt[...] = fresh
        else:
            out[...] = fresh.T

    for k in range(1, n):
        psf_copy(k).wait_send()
        cam_copy(k).wait_send()
    for it in range(ITERS):
        finish(x_copy, it)
        finish(r_copy, it)


def power_of_two(a):
    return a & (a - 1) == 0


def fused_shards(dims, camera_rows, estimate, psf_bank, psf_owner, view_mask):
    n, brick, zd, rows, cols = dims
    lr = rows // n
    cells = zd * rows
    vmem = pl.BlockSpec(memory_space=pltpu.VMEM)
    smem = pl.BlockSpec(memory_space=pltpu.SMEM)
    result = pl.pallas_call(
        functools.partial(fused, dims),
        out_shape=jax.ShapeDtypeStruct((cells, cols), F32),
        in_specs=[vmem, vmem, vmem, smem, smem],
        out_specs=vmem,
        scratch_shapes=[
            pltpu.VMEM((16, 128), F32),
            pltpu.VMEM((n, 3, V, psf_bank.shape[-1]), F32),
            pltpu.VMEM((n, V * zd * lr, cols), BF16),
            pltpu.VMEM((V, cols, cells), F32),
            pltpu.VMEM((ITERS, 2 * EDGE, cells), BF16),
            pltpu.VMEM((ITERS, 2 * EDGE, cells), BF16),
            pltpu.VMEM((ITERS, V, 2 * EDGE, cells), BF16),
            pltpu.VMEM((ITERS, V, 2 * EDGE, cells), BF16),
            pltpu.VMEM((V, cells, cells), BF16),
            pltpu.VMEM((V, cells, cells), BF16),
            pltpu.VMEM((4, V, cols, cols), BF16),
            pltpu.VMEM((2, V, cols, cols), BF16),
            pltpu.VMEM((cols, cells), F32),
            pltpu.SemaphoreType.DMA((2, n)),
            pltpu.SemaphoreType.DMA((2, n)),
            pltpu.SemaphoreType.DMA((2, ITERS, 2)),
            pltpu.SemaphoreType.DMA((2, ITERS, 2)),
            pltpu.SemaphoreType.DMA,
        ],
        compiler_params=pltpu.CompilerParams(
            collective_id=0, has_side_effects=True, vmem_limit_bytes=32 * 1024 * 1024
        ),
    )(
        camera_rows.reshape(V * zd * lr, n * cols),
        estimate.reshape(cells, cols),
        psf_bank.transpose(0, 2, 1, 3),
        psf_owner,
        view_mask.T,
    )
    return result.reshape(zd, rows, cols)


def solution(mesh):
    n = mesh.shape["plane"] * mesh.shape["brick"]

    def shards_of(camera_rows, estimate, psf_bank, psf_owner, view_mask):
        zd, rows, cols = estimate.shape
        lr = camera_rows.shape[2]
        small = (
            zd * rows == 256
            and cols == 128
            and psf_bank.shape[-1] == 2 * RADIUS + 1
            and lr * n == rows
            and zd % 8 == 0
            and zd * lr % 16 == 0
            and power_of_two(zd)
            and power_of_two(lr)
        )
        if not small:
            return shards(camera_rows, estimate, psf_bank, psf_owner, view_mask)
        dims = (n, mesh.shape["brick"], zd, rows, cols)
        return fused_shards(dims, camera_rows, estimate, psf_bank, psf_owner, view_mask)

    return jax.shard_map(
        shards_of,
        mesh=mesh,
        in_specs=(
            P(None, "slab", ("plane", "brick"), None),
            P("slab", None, ("plane", "brick")),
            P(("slab", "plane", "brick"), None, None, None),
            P("slab"),
            P("slab", None),
        ),
        out_specs=P("slab", None, ("plane", "brick")),
        check_vma=False,
    )
```

```python
import functools

import jax
import jax.numpy as jnp
from jax import lax
from jax.experimental import pallas as pl
from jax.experimental.pallas import tpu as pltpu
from jax.sharding import PartitionSpec as P

V = 4
RADIUS = 15
ITERS = 2
EDGE = 16


BACKGROUND = 0.1
HIGHEST = lax.Precision.HIGHEST
F32 = jnp.float32
BF16 = jnp.bfloat16
def padded_2(cells, sides, width):
    for axis, dim in sides:
        count = lax.axis_size(axis)
        ends = count - 1
        head = lax.slice_in_dim(cells, 0, width, axis=dim)
        tail = lax.slice_in_dim(cells, cells.shape[dim] - width, cells.shape[dim], axis=dim)
        cells = jnp.concatenate(
            [
                lax.ppermute(tail, axis, [(i, (i + 1) % count) for i in range(ends)]),
                cells,
                lax.ppermute(head, axis, [((i + 1) % count, i) for i in range(ends)]),
            ],
            axis=dim,
        )
    return cells


def banded(profiles, size_in, size_out, offset):
    tap_count = profiles.shape[-1]
    centre = tap_count // 2
    lag_index = (
        jnp.arange(size_in, dtype=jnp.int32)[:, None]
        - jnp.arange(size_out, dtype=jnp.int32)[None, :]
        - offset
        + centre
    )
    one_hot = (
        lag_index[:, :, None] == jnp.arange(tap_count, dtype=jnp.int32)[None, None, :]
    ).astype(jnp.float32)
    return jnp.einsum("ijt,vt->vij", one_hot, profiles, precision=HIGHEST)


def across_columns(volume, band_x):
    if volume.ndim == 3:
        return jnp.einsum("zyi,vij->vzyj", volume, band_x, precision=HIGHEST)
    return jnp.einsum("vzyi,vij->vzyj", volume, band_x, precision=HIGHEST)


def across_rows(volume, band_y):
    view_count, depth_count, row_count, col_count = volume.shape
    block_rows = band_y.shape[2]
    margin = (band_y.shape[1] - block_rows) // 2
    pieces = volume.reshape(view_count, depth_count, row_count // block_rows, block_rows, col_count)
    blanks = jnp.zeros((view_count, depth_count, 1, margin, col_count), jnp.float32)
    before = jnp.concatenate([blanks, pieces[:, :, :-1, block_rows - margin :, :]], axis=2)
    behind = jnp.concatenate([pieces[:, :, 1:, :margin, :], blanks], axis=2)
    windows = jnp.concatenate([before, pieces, behind], axis=3)
    result = jnp.einsum("vzqic,vij->vzqjc", windows, band_y, precision=HIGHEST)
    return result.reshape(view_count, depth_count, row_count, col_count)


def across_depth(volume, band_z):
    return jnp.einsum("vzyc,vzw->vwyc", volume, band_z, precision=HIGHEST)


def separable(volume, bands):
    return across_depth(across_rows(across_columns(volume, bands[0]), bands[1]), bands[2])


def shards(camera_rows, estimate, psf_bank, psf_owner, view_mask):
    regrouped = lax.all_to_all(
        camera_rows, ("plane", "brick"), split_axis=3, concat_axis=2, tiled=True
    )
    position = lax.axis_index(("plane", "brick"))
    brick_ids = jnp.arange(psf_owner.shape[0], dtype=jnp.int32)
    is_mine = brick_ids == position
    owner_id = jnp.sum(jnp.where(is_mine, psf_owner, 0))
    observed = jnp.sum(jnp.where(is_mine[:, None], view_mask, 0), axis=0) > 0
    fitted = lax.all_gather(psf_bank, ("plane", "brick"), axis=0, tiled=True)
    chosen = (brick_ids == owner_id).astype(jnp.float32)
    kernels = jnp.einsum("b,bvat->vat", chosen, fitted, precision=HIGHEST)
    kernels = kernels / jnp.sum(kernels, axis=-1, keepdims=True)
    flipped = kernels[:, :, ::-1]
    depth_size = estimate.shape[0]
    row_size = estimate.shape[1]
    col_size = estimate.shape[2]
    block_size = 128 if row_size % 128 == 0 else row_size

    def make_bands(profiles):
        return (
            banded(profiles[:, 2], col_size + 2 * RADIUS, col_size, RADIUS),
            banded(profiles[:, 1], block_size + 2 * RADIUS, block_size, RADIUS),
            banded(profiles[:, 0], depth_size, depth_size, 0),
        )

    blur_bands = make_bands(kernels)
    back_bands = make_bands(flipped)
    current = estimate
    for iteration in range(ITERS):
        padded = padded_2(current.astype(jnp.bfloat16), ((("plane", "brick"), 2),), RADIUS).astype(
            current.dtype
        )
        blurred = separable(padded, blur_bands)
        quotient = jnp.where(
            observed[:, None, None, None],
            regrouped.astype(jnp.float32) / (blurred + BACKGROUND),
            0.0,
        )
        quotient_wide = padded_2(
            quotient.astype(jnp.bfloat16), ((("plane", "brick"), 3),), RADIUS
        ).astype(quotient.dtype)
        corrected = separable(quotient_wide, back_bands)
        factor = jnp.sum(jnp.where(observed[:, None, None, None], corrected, 1.0), axis=0) / V
        current = current * factor
    return current


def split(a):
    hi = a.astype(BF16)
    return hi, (a - hi.astype(F32)).astype(BF16)


def dot(a, b, nt=False):
    dims = (((1,), (1 if nt else 0,)), ((), ()))
    return lax.dot_general(a, b, dims, preferred_element_type=F32)


def dot3(a, b, nt=False):
    return dot(a[0], b[0], nt) + (dot(a[0], b[1], nt) + dot(a[1], b[0], nt))


def dot2(a, b, nt=False):
    return dot(a, b[0], nt) + dot(a, b[1], nt)


def exact(a, b):
    return lax.dot_general(a, b, (((1,), (0,)), ((), ())), precision=HIGHEST, preferred_element_type=F32)


def fused(
    dims, cam, est, psf, owner, mask, out,
    taps, gath, camrecv, camt, xsend, xhalo, rsend, rhalo, kbh, kbl, abl, aback, xt,
    psf_sems, cam_sems, x_sems, r_sems, own_sem,
):
    n, brick, zd, rows, cols = dims
    lr = rows // n
    part = zd * lr
    cells = zd * rows
    taps_n = psf.shape[-1]
    me = lax.axis_index("plane") * brick + lax.axis_index("brick")

    def device(t):
        return {"plane": lax.div(t, brick), "brick": lax.rem(t, brick)}

    def peer(k):
        return lax.rem(me + k, n)

    barrier = pltpu.get_barrier_semaphore()
    for k in range(1, n):
        pl.semaphore_signal(barrier, inc=1, device_id=device(peer(k)), device_id_type=pl.DeviceIdType.MESH)

    has_left = me > 0
    has_right = me < n - 1
    zero_edge = jnp.zeros((EDGE, cells), BF16)

    @pl.when(me == 0)
    def _():
        for it in range(ITERS):
            xhalo[it, 0:EDGE, :] = zero_edge
            for v in range(V):
                rhalo[it, v, 0:EDGE, :] = zero_edge

    @pl.when(me == n - 1)
    def _():
        for it in range(ITERS):
            xhalo[it, EDGE:, :] = zero_edge
            for v in range(V):
                rhalo[it, v, EDGE:, :] = zero_edge

    def x_copy(it, side):
        rows_of = pl.ds(side * EDGE, EDGE)
        return pltpu.make_async_remote_copy(
            src_ref=xsend.at[it, rows_of], dst_ref=xhalo.at[it, rows_of],
            send_sem=x_sems.at[0, it, side], recv_sem=x_sems.at[1, it, side],
            device_id=device(lax.rem(me + n + 1 - 2 * side, n)), device_id_type=pl.DeviceIdType.MESH,
        )

    def r_copy(it, side):
        rows_of = pl.ds(side * EDGE, EDGE)
        return pltpu.make_async_remote_copy(
            src_ref=rsend.at[it, :, rows_of], dst_ref=rhalo.at[it, :, rows_of],
            send_sem=r_sems.at[0, it, side], recv_sem=r_sems.at[1, it, side],
            device_id=device(lax.rem(me + n + 1 - 2 * side, n)), device_id_type=pl.DeviceIdType.MESH,
        )

    def start(make, it):
        @pl.when(has_right)
        def _():
            make(it, 0).start()

        @pl.when(has_left)
        def _():
            make(it, 1).start()

    def arrive(make, it):
        @pl.when(has_left)
        def _():
            make(it, 0).wait_recv()

        @pl.when(has_right)
        def _():
            make(it, 1).wait_recv()

    def finish(make, it):
        @pl.when(has_right)
        def _():
            make(it, 0).wait_send()

        @pl.when(has_left)
        def _():
            make(it, 1).wait_send()

    def psf_copy(k):
        return pltpu.make_async_remote_copy(
            src_ref=psf.at[0], dst_ref=gath.at[me],
            send_sem=psf_sems.at[0, k], recv_sem=psf_sems.at[1, k],
            device_id=device(peer(k)), device_id_type=pl.DeviceIdType.MESH,
        )

    def cam_copy(k):
        return pltpu.make_async_remote_copy(
            src_ref=cam.at[:, pl.ds(pl.multiple_of(peer(k) * cols, cols), cols)], dst_ref=camrecv.at[me],
            send_sem=cam_sems.at[0, k], recv_sem=cam_sems.at[1, k],
            device_id=device(peer(k)), device_id_type=pl.DeviceIdType.MESH,
        )

    own = pltpu.make_async_copy(
        cam.at[:, pl.ds(pl.multiple_of(me * cols, cols), cols)], camrecv.at[me], own_sem
    )
    own.start()
    x0 = est[...].T
    xt[...] = x0
    xsend[0, 0:EDGE, :] = x0[cols - EDGE :, :].astype(BF16)
    xsend[0, EDGE:, :] = x0[:EDGE, :].astype(BF16)
    gath[me] = psf[0]

    pl.semaphore_wait(barrier, n - 1)
    far_first = list(range(1, n))
    for k in far_first:
        psf_copy(k).start()
    start(x_copy, 0)
    for k in far_first:
        cam_copy(k).start()

    lane = lax.broadcasted_iota(jnp.int32, (128, cells), 1)
    line = lax.broadcasted_iota(jnp.int32, (128, cells), 0)
    y_of = lax.shift_right_logical(lane, part.bit_length() - 1) * lr + (lane & (lr - 1))
    z_of = lax.shift_right_logical(lane, lr.bit_length() - 1) & (zd - 1)
    pick_y = (y_of == line).astype(F32)
    pick_z = (z_of == line).astype(F32)
    flip = (
        lax.broadcasted_iota(jnp.int32, (128, 128), 0) + lax.broadcasted_iota(jnp.int32, (128, 128), 1)
        == taps_n - 1
    ).astype(F32)
    taps[...] = jnp.zeros_like(taps)

    for k in range(1, n):
        psf_copy(k).wait_recv()
    block = gath[owner[me]]
    for a in range(3):
        taps[a * V : (a + 1) * V, 0:taps_n] = block[a]
    kernels = taps[...]
    total = jnp.sum(kernels, axis=-1, keepdims=True)
    kernels = kernels / jnp.where(total > 0.0, total, 1.0)
    flipped = exact(kernels, flip)

    def toeplitz(row, height, width):
        if width > 128:
            row = jnp.concatenate([row, jnp.zeros((1, width - 128), F32)], axis=1)
        return pltpu.roll(
            jnp.broadcast_to(row, (height, width)), width - RADIUS, 1, stride=1, stride_axis=0
        )

    lines_y = jnp.concatenate([toeplitz(flipped[V + v : V + v + 1], rows, 128) for v in range(V)], axis=0)
    lines_z = jnp.concatenate([toeplitz(flipped[v : v + 1], zd, 128) for v in range(V)], axis=0)
    wide_y = exact(lines_y, pick_y)
    wide_z = exact(lines_z, pick_z)
    seen = [mask[v, me] > 0 for v in range(V)]
    back_edge = jnp.zeros((cols, 128), F32)
    for v in range(V):
        for z in range(zd):
            piece = wide_y[v * rows : (v + 1) * rows] * wide_z[v * zd + z : v * zd + z + 1]
            hi, lo = split(piece)
            kbh[v, z * rows : (z + 1) * rows, :] = hi
            kbl[v, z * rows : (z + 1) * rows, :] = lo
        band = toeplitz(kernels[2 * V + v : 2 * V + v + 1], cols, 2 * cols)
        hi, lo = split(band[:, :cols])
        abl[0, v] = hi
        abl[1, v] = lo
        hi, lo = split(pltpu.roll(band[:, cols:], EDGE, 1))
        abl[2, v] = hi
        abl[3, v] = lo
        band = jnp.where(seen[v], toeplitz(flipped[2 * V + v : 2 * V + v + 1], cols, 2 * cols), 0.0)
        hi, lo = split(band[:, :cols])
        aback[0, :, v * cols : (v + 1) * cols] = hi
        aback[1, :, v * cols : (v + 1) * cols] = lo
        back_edge = back_edge + pltpu.roll(band[:, cols:], (EDGE + 2 * EDGE * v) % 128, 1)
    back_edge = split(back_edge)
    unseen = functools.reduce(jnp.add, [jnp.where(s, 0.0, 1.0) for s in seen])

    for it in range(ITERS):
        x = split(xt[...])
        blurred = []
        for v in range(V):
            spread = split(dot3(x, (kbh[v], kbl[v])))
            blurred.append(dot3((abl[0, v], abl[1, v]), spread))
        arrive(x_copy, it)
        edge = xhalo[it]
        for v in range(V):
            spread = split(dot2(edge, (kbh[v], kbl[v])))
            blurred[v] = blurred[v] + dot3((abl[2, v, :, 0 : 2 * EDGE], abl[3, v, :, 0 : 2 * EDGE]), spread)
        if it == 0:
            for k in range(1, n):
                cam_copy(k).wait_recv()
            own.wait()
            for v in range(V):
                tile = camrecv[:, v * part : (v + 1) * part, :].reshape(cells, cols)
                camt[v] = tile.astype(F32).T
        ratios = []
        for v in range(V):
            ratio = jnp.where(seen[v], camt[v] / (blurred[v] + BACKGROUND), 0.0)
            rsend[it, v, 0:EDGE, :] = ratio[cols - EDGE :, :].astype(BF16)
            rsend[it, v, EDGE:, :] = ratio[:EDGE, :].astype(BF16)
            ratios.append(ratio)
        start(r_copy, it)
        spread = [split(dot3(split(ratios[v]), (kbh[v], kbl[v]), nt=True)) for v in range(V)]
        hi = jnp.concatenate([a for a, _ in spread], axis=0)
        lo = jnp.concatenate([b for _, b in spread], axis=0)
        total = dot3((aback[0], aback[1]), (hi, lo))
        arrive(r_copy, it)
        spread = [dot2(rhalo[it, v], (kbh[v], kbl[v]), nt=True) for v in range(V)]
        total = total + dot3(back_edge, split(jnp.concatenate(spread, axis=0)))
        fresh = xt[...] * ((total + unseen) * (1.0 / V))
        if it < ITERS - 1:
            xsend[it + 1, 0:EDGE, :] = fresh[cols - EDGE :, :].astype(BF16)
            xsend[it + 1, EDGE:, :] = fresh[:EDGE, :].astype(BF16)
            start(x_copy, it + 1)
            xt[...] = fresh
        else:
            out[...] = fresh.T

    for k in range(1, n):
        psf_copy(k).wait_send()
        cam_copy(k).wait_send()
    for it in range(ITERS):
        finish(x_copy, it)
        finish(r_copy, it)


def power_of_two(a):
    return a & (a - 1) == 0


def fused_shards(dims, camera_rows, estimate, psf_bank, psf_owner, view_mask):
    n, brick, zd, rows, cols = dims
    lr = rows // n
    cells = zd * rows
    vmem = pl.BlockSpec(memory_space=pltpu.VMEM)
    smem = pl.BlockSpec(memory_space=pltpu.SMEM)
    result = pl.pallas_call(
        functools.partial(fused, dims),
        out_shape=jax.ShapeDtypeStruct((cells, cols), F32),
        in_specs=[vmem, vmem, vmem, smem, smem],
        out_specs=vmem,
        scratch_shapes=[
            pltpu.VMEM((16, 128), F32),
            pltpu.VMEM((n, 3, V, psf_bank.shape[-1]), F32),
            pltpu.VMEM((n, V * zd * lr, cols), BF16),
            pltpu.VMEM((V, cols, cells), F32),
            pltpu.VMEM((ITERS, 2 * EDGE, cells), BF16),
            pltpu.VMEM((ITERS, 2 * EDGE, cells), BF16),
            pltpu.VMEM((ITERS, V, 2 * EDGE, cells), BF16),
            pltpu.VMEM((ITERS, V, 2 * EDGE, cells), BF16),
            pltpu.VMEM((V, cells, cells), BF16),
            pltpu.VMEM((V, cells, cells), BF16),
            pltpu.VMEM((4, V, cols, cols), BF16),
            pltpu.VMEM((2, cols, V * cols), BF16),
            pltpu.VMEM((cols, cells), F32),
            pltpu.SemaphoreType.DMA((2, n)),
            pltpu.SemaphoreType.DMA((2, n)),
            pltpu.SemaphoreType.DMA((2, ITERS, 2)),
            pltpu.SemaphoreType.DMA((2, ITERS, 2)),
            pltpu.SemaphoreType.DMA,
        ],
        compiler_params=pltpu.CompilerParams(
            collective_id=0, has_side_effects=True, vmem_limit_bytes=32 * 1024 * 1024
        ),
    )(
        camera_rows.reshape(V * zd * lr, n * cols),
        estimate.reshape(cells, cols),
        psf_bank.transpose(0, 2, 1, 3),
        psf_owner,
        view_mask.T,
    )
    return result.reshape(zd, rows, cols)


def solution(mesh):
    n = mesh.shape["plane"] * mesh.shape["brick"]

    def shards_of(camera_rows, estimate, psf_bank, psf_owner, view_mask):
        zd, rows, cols = estimate.shape
        lr = camera_rows.shape[2]
        small = (
            zd * rows == 256
            and cols == 128
            and psf_bank.shape[-1] == 2 * RADIUS + 1
            and lr * n == rows
            and zd % 8 == 0
            and zd * lr % 16 == 0
            and power_of_two(zd)
            and power_of_two(lr)
        )
        if not small:
            return shards(camera_rows, estimate, psf_bank, psf_owner, view_mask)
        dims = (n, mesh.shape["brick"], zd, rows, cols)
        return fused_shards(dims, camera_rows, estimate, psf_bank, psf_owner, view_mask)

    return jax.shard_map(
        shards_of,
        mesh=mesh,
        in_specs=(
            P(None, "slab", ("plane", "brick"), None),
            P("slab", None, ("plane", "brick")),
            P(("slab", "plane", "brick"), None, None, None),
            P("slab"),
            P("slab", None),
        ),
        out_specs=P("slab", None, ("plane", "brick")),
        check_vma=False,
    )
```

```python
import functools

import jax
import jax.numpy as jnp
from jax import lax
from jax.experimental import pallas as pl
from jax.experimental.pallas import tpu as pltpu
from jax.sharding import PartitionSpec as P

V = 4
RADIUS = 15
ITERS = 2
EDGE = 16


BACKGROUND = 0.1
HIGHEST = lax.Precision.HIGHEST
F32 = jnp.float32
BF16 = jnp.bfloat16
def padded_2(cells, sides, width):
    for axis, dim in sides:
        count = lax.axis_size(axis)
        ends = count - 1
        head = lax.slice_in_dim(cells, 0, width, axis=dim)
        tail = lax.slice_in_dim(cells, cells.shape[dim] - width, cells.shape[dim], axis=dim)
        cells = jnp.concatenate(
            [
                lax.ppermute(tail, axis, [(i, (i + 1) % count) for i in range(ends)]),
                cells,
                lax.ppermute(head, axis, [((i + 1) % count, i) for i in range(ends)]),
            ],
            axis=dim,
        )
    return cells


def banded(profiles, size_in, size_out, offset):
    tap_count = profiles.shape[-1]
    centre = tap_count // 2
    lag_index = (
        jnp.arange(size_in, dtype=jnp.int32)[:, None]
        - jnp.arange(size_out, dtype=jnp.int32)[None, :]
        - offset
        + centre
    )
    one_hot = (
        lag_index[:, :, None] == jnp.arange(tap_count, dtype=jnp.int32)[None, None, :]
    ).astype(jnp.float32)
    return jnp.einsum("ijt,vt->vij", one_hot, profiles, precision=HIGHEST)


def across_columns(volume, band_x):
    if volume.ndim == 3:
        return jnp.einsum("zyi,vij->vzyj", volume, band_x, precision=HIGHEST)
    return jnp.einsum("vzyi,vij->vzyj", volume, band_x, precision=HIGHEST)


def across_rows(volume, band_y):
    view_count, depth_count, row_count, col_count = volume.shape
    block_rows = band_y.shape[2]
    margin = (band_y.shape[1] - block_rows) // 2
    pieces = volume.reshape(view_count, depth_count, row_count // block_rows, block_rows, col_count)
    blanks = jnp.zeros((view_count, depth_count, 1, margin, col_count), jnp.float32)
    before = jnp.concatenate([blanks, pieces[:, :, :-1, block_rows - margin :, :]], axis=2)
    behind = jnp.concatenate([pieces[:, :, 1:, :margin, :], blanks], axis=2)
    windows = jnp.concatenate([before, pieces, behind], axis=3)
    result = jnp.einsum("vzqic,vij->vzqjc", windows, band_y, precision=HIGHEST)
    return result.reshape(view_count, depth_count, row_count, col_count)


def across_depth(volume, band_z):
    return jnp.einsum("vzyc,vzw->vwyc", volume, band_z, precision=HIGHEST)


def separable(volume, bands):
    return across_depth(across_rows(across_columns(volume, bands[0]), bands[1]), bands[2])


def shards(camera_rows, estimate, psf_bank, psf_owner, view_mask):
    regrouped = lax.all_to_all(
        camera_rows, ("plane", "brick"), split_axis=3, concat_axis=2, tiled=True
    )
    position = lax.axis_index(("plane", "brick"))
    brick_ids = jnp.arange(psf_owner.shape[0], dtype=jnp.int32)
    is_mine = brick_ids == position
    owner_id = jnp.sum(jnp.where(is_mine, psf_owner, 0))
    observed = jnp.sum(jnp.where(is_mine[:, None], view_mask, 0), axis=0) > 0
    fitted = lax.all_gather(psf_bank, ("plane", "brick"), axis=0, tiled=True)
    chosen = (brick_ids == owner_id).astype(jnp.float32)
    kernels = jnp.einsum("b,bvat->vat", chosen, fitted, precision=HIGHEST)
    kernels = kernels / jnp.sum(kernels, axis=-1, keepdims=True)
    flipped = kernels[:, :, ::-1]
    depth_size = estimate.shape[0]
    row_size = estimate.shape[1]
    col_size = estimate.shape[2]
    block_size = 128 if row_size % 128 == 0 else row_size

    def make_bands(profiles):
        return (
            banded(profiles[:, 2], col_size + 2 * RADIUS, col_size, RADIUS),
            banded(profiles[:, 1], block_size + 2 * RADIUS, block_size, RADIUS),
            banded(profiles[:, 0], depth_size, depth_size, 0),
        )

    blur_bands = make_bands(kernels)
    back_bands = make_bands(flipped)
    current = estimate
    for iteration in range(ITERS):
        padded = padded_2(current.astype(jnp.bfloat16), ((("plane", "brick"), 2),), RADIUS).astype(
            current.dtype
        )
        blurred = separable(padded, blur_bands)
        quotient = jnp.where(
            observed[:, None, None, None],
            regrouped.astype(jnp.float32) / (blurred + BACKGROUND),
            0.0,
        )
        quotient_wide = padded_2(
            quotient.astype(jnp.bfloat16), ((("plane", "brick"), 3),), RADIUS
        ).astype(quotient.dtype)
        corrected = separable(quotient_wide, back_bands)
        factor = jnp.sum(jnp.where(observed[:, None, None, None], corrected, 1.0), axis=0) / V
        current = current * factor
    return current


def split(a):
    hi = a.astype(BF16)
    return hi, (a - hi.astype(F32)).astype(BF16)


def dot(a, b, nt=False):
    dims = (((1,), (1 if nt else 0,)), ((), ()))
    return lax.dot_general(a, b, dims, preferred_element_type=F32)


def dot3(a, b, nt=False):
    return dot(a[0], b[0], nt) + (dot(a[0], b[1], nt) + dot(a[1], b[0], nt))


def dot2(a, b, nt=False):
    return dot(a, b[0], nt) + dot(a, b[1], nt)


def exact(a, b):
    return lax.dot_general(a, b, (((1,), (0,)), ((), ())), precision=HIGHEST, preferred_element_type=F32)


def fused(
    dims, cam, est, psf, owner, mask, out,
    taps, gath, camrecv, camt, xsend, xhalo, rsend, rhalo, kbh, kbl, abl, aback, xt,
    psf_sems, cam_sems, x_sems, r_sems, own_sem,
):
    n, brick, zd, rows, cols = dims
    lr = rows // n
    part = zd * lr
    cells = zd * rows
    taps_n = psf.shape[-1]
    me = lax.axis_index("plane") * brick + lax.axis_index("brick")

    def device(t):
        return {"plane": lax.div(t, brick), "brick": lax.rem(t, brick)}

    def peer(k):
        return lax.rem(me + k, n)

    barrier = pltpu.get_barrier_semaphore()
    for k in range(1, n):
        pl.semaphore_signal(barrier, inc=1, device_id=device(peer(k)), device_id_type=pl.DeviceIdType.MESH)

    has_left = me > 0
    has_right = me < n - 1
    zero_edge = jnp.zeros((EDGE, cells), BF16)

    @pl.when(me == 0)
    def _():
        for it in range(ITERS):
            xhalo[it, 0:EDGE, :] = zero_edge
            for v in range(V):
                rhalo[it, v, 0:EDGE, :] = zero_edge

    @pl.when(me == n - 1)
    def _():
        for it in range(ITERS):
            xhalo[it, EDGE:, :] = zero_edge
            for v in range(V):
                rhalo[it, v, EDGE:, :] = zero_edge

    def x_copy(it, side):
        rows_of = pl.ds(side * EDGE, EDGE)
        return pltpu.make_async_remote_copy(
            src_ref=xsend.at[it, rows_of], dst_ref=xhalo.at[it, rows_of],
            send_sem=x_sems.at[0, it, side], recv_sem=x_sems.at[1, it, side],
            device_id=device(lax.rem(me + n + 1 - 2 * side, n)), device_id_type=pl.DeviceIdType.MESH,
        )

    def r_copy(it, side):
        rows_of = pl.ds(side * EDGE, EDGE)
        return pltpu.make_async_remote_copy(
            src_ref=rsend.at[it, :, rows_of], dst_ref=rhalo.at[it, :, rows_of],
            send_sem=r_sems.at[0, it, side], recv_sem=r_sems.at[1, it, side],
            device_id=device(lax.rem(me + n + 1 - 2 * side, n)), device_id_type=pl.DeviceIdType.MESH,
        )

    def start(make, it):
        @pl.when(has_right)
        def _():
            make(it, 0).start()

        @pl.when(has_left)
        def _():
            make(it, 1).start()

    def arrive(make, it):
        @pl.when(has_left)
        def _():
            make(it, 0).wait_recv()

        @pl.when(has_right)
        def _():
            make(it, 1).wait_recv()

    def finish(make, it):
        @pl.when(has_right)
        def _():
            make(it, 0).wait_send()

        @pl.when(has_left)
        def _():
            make(it, 1).wait_send()

    def psf_copy(k):
        return pltpu.make_async_remote_copy(
            src_ref=psf.at[0], dst_ref=gath.at[me],
            send_sem=psf_sems.at[0, k], recv_sem=psf_sems.at[1, k],
            device_id=device(peer(k)), device_id_type=pl.DeviceIdType.MESH,
        )

    def cam_copy(k):
        return pltpu.make_async_remote_copy(
            src_ref=cam.at[:, pl.ds(pl.multiple_of(peer(k) * cols, cols), cols)], dst_ref=camrecv.at[me],
            send_sem=cam_sems.at[0, k], recv_sem=cam_sems.at[1, k],
            device_id=device(peer(k)), device_id_type=pl.DeviceIdType.MESH,
        )

    own = pltpu.make_async_copy(
        cam.at[:, pl.ds(pl.multiple_of(me * cols, cols), cols)], camrecv.at[me], own_sem
    )
    own.start()

    pl.semaphore_wait(barrier, n - 1)
    far_first = list(range(1, n))
    for k in far_first:
        psf_copy(k).start()
    for k in far_first:
        cam_copy(k).start()
    x0 = est[...].T
    xt[...] = x0
    xsend[0, 0:EDGE, :] = x0[cols - EDGE :, :].astype(BF16)
    xsend[0, EDGE:, :] = x0[:EDGE, :].astype(BF16)
    gath[me] = psf[0]
    start(x_copy, 0)

    lane = lax.broadcasted_iota(jnp.int32, (128, cells), 1)
    line = lax.broadcasted_iota(jnp.int32, (128, cells), 0)
    y_of = lax.shift_right_logical(lane, part.bit_length() - 1) * lr + (lane & (lr - 1))
    z_of = lax.shift_right_logical(lane, lr.bit_length() - 1) & (zd - 1)
    pick_y = (y_of == line).astype(F32)
    pick_z = (z_of == line).astype(F32)
    flip = (
        lax.broadcasted_iota(jnp.int32, (128, 128), 0) + lax.broadcasted_iota(jnp.int32, (128, 128), 1)
        == taps_n - 1
    ).astype(F32)
    taps[...] = jnp.zeros_like(taps)

    for k in range(1, n):
        psf_copy(k).wait_recv()
    block = gath[owner[me]]
    for a in range(3):
        taps[a * V : (a + 1) * V, 0:taps_n] = block[a]
    kernels = taps[...]
    total = jnp.sum(kernels, axis=-1, keepdims=True)
    kernels = kernels / jnp.where(total > 0.0, total, 1.0)
    flipped = exact(kernels, flip)

    def toeplitz(row, height, width):
        if width > 128:
            row = jnp.concatenate([row, jnp.zeros((1, width - 128), F32)], axis=1)
        return pltpu.roll(
            jnp.broadcast_to(row, (height, width)), width - RADIUS, 1, stride=1, stride_axis=0
        )

    lines_y = jnp.concatenate([toeplitz(flipped[V + v : V + v + 1], rows, 128) for v in range(V)], axis=0)
    lines_z = jnp.concatenate([toeplitz(flipped[v : v + 1], zd, 128) for v in range(V)], axis=0)
    wide_y = exact(lines_y, pick_y)
    wide_z = exact(lines_z, pick_z)
    seen = [mask[v, me] > 0 for v in range(V)]
    back_edge = jnp.zeros((cols, 128), F32)
    for v in range(V):
        for z in range(zd):
            piece = wide_y[v * rows : (v + 1) * rows] * wide_z[v * zd + z : v * zd + z + 1]
            hi, lo = split(piece)
            kbh[v, z * rows : (z + 1) * rows, :] = hi
            kbl[v, z * rows : (z + 1) * rows, :] = lo
        band = toeplitz(kernels[2 * V + v : 2 * V + v + 1], cols, 2 * cols)
        hi, lo = split(band[:, :cols])
        abl[0, v] = hi
        abl[1, v] = lo
        hi, lo = split(pltpu.roll(band[:, cols:], EDGE, 1))
        abl[2, v] = hi
        abl[3, v] = lo
        band = jnp.where(seen[v], toeplitz(flipped[2 * V + v : 2 * V + v + 1], cols, 2 * cols), 0.0)
        hi, lo = split(band[:, :cols])
        aback[0, :, v * cols : (v + 1) * cols] = hi
        aback[1, :, v * cols : (v + 1) * cols] = lo
        back_edge = back_edge + pltpu.roll(band[:, cols:], (EDGE + 2 * EDGE * v) % 128, 1)
    back_edge = split(back_edge)
    unseen = functools.reduce(jnp.add, [jnp.where(s, 0.0, 1.0) for s in seen])

    for it in range(ITERS):
        x = split(xt[...])
        blurred = []
        for v in range(V):
            spread = split(dot3(x, (kbh[v], kbl[v])))
            blurred.append(dot3((abl[0, v], abl[1, v]), spread))
        arrive(x_copy, it)
        edge = xhalo[it]
        for v in range(V):
            spread = split(dot2(edge, (kbh[v], kbl[v])))
            blurred[v] = blurred[v] + dot3((abl[2, v, :, 0 : 2 * EDGE], abl[3, v, :, 0 : 2 * EDGE]), spread)
        if it == 0:
            for k in range(1, n):
                cam_copy(k).wait_recv()
            own.wait()
            for v in range(V):
                tile = camrecv[:, v * part : (v + 1) * part, :].reshape(cells, cols)
                camt[v] = tile.astype(F32).T
        ratios = []
        for v in range(V):
            ratio = jnp.where(seen[v], camt[v] / (blurred[v] + BACKGROUND), 0.0)
            rsend[it, v, 0:EDGE, :] = ratio[cols - EDGE :, :].astype(BF16)
            rsend[it, v, EDGE:, :] = ratio[:EDGE, :].astype(BF16)
            ratios.append(ratio)
        start(r_copy, it)
        spread = [split(dot3(split(ratios[v]), (kbh[v], kbl[v]), nt=True)) for v in range(V)]
        hi = jnp.concatenate([a for a, _ in spread], axis=0)
        lo = jnp.concatenate([b for _, b in spread], axis=0)
        total = dot3((aback[0], aback[1]), (hi, lo))
        arrive(r_copy, it)
        spread = [dot2(rhalo[it, v], (kbh[v], kbl[v]), nt=True) for v in range(V)]
        total = total + dot3(back_edge, split(jnp.concatenate(spread, axis=0)))
        fresh = xt[...] * ((total + unseen) * (1.0 / V))
        if it < ITERS - 1:
            xsend[it + 1, 0:EDGE, :] = fresh[cols - EDGE :, :].astype(BF16)
            xsend[it + 1, EDGE:, :] = fresh[:EDGE, :].astype(BF16)
            start(x_copy, it + 1)
            xt[...] = fresh
        else:
            out[...] = fresh.T

    for k in range(1, n):
        psf_copy(k).wait_send()
        cam_copy(k).wait_send()
    for it in range(ITERS):
        finish(x_copy, it)
        finish(r_copy, it)


def power_of_two(a):
    return a & (a - 1) == 0


def fused_shards(dims, camera_rows, estimate, psf_bank, psf_owner, view_mask):
    n, brick, zd, rows, cols = dims
    lr = rows // n
    cells = zd * rows
    vmem = pl.BlockSpec(memory_space=pltpu.VMEM)
    smem = pl.BlockSpec(memory_space=pltpu.SMEM)
    result = pl.pallas_call(
        functools.partial(fused, dims),
        out_shape=jax.ShapeDtypeStruct((cells, cols), F32),
        in_specs=[vmem, vmem, vmem, smem, smem],
        out_specs=vmem,
        scratch_shapes=[
            pltpu.VMEM((16, 128), F32),
            pltpu.VMEM((n, 3, V, psf_bank.shape[-1]), F32),
            pltpu.VMEM((n, V * zd * lr, cols), BF16),
            pltpu.VMEM((V, cols, cells), F32),
            pltpu.VMEM((ITERS, 2 * EDGE, cells), BF16),
            pltpu.VMEM((ITERS, 2 * EDGE, cells), BF16),
            pltpu.VMEM((ITERS, V, 2 * EDGE, cells), BF16),
            pltpu.VMEM((ITERS, V, 2 * EDGE, cells), BF16),
            pltpu.VMEM((V, cells, cells), BF16),
            pltpu.VMEM((V, cells, cells), BF16),
            pltpu.VMEM((4, V, cols, cols), BF16),
            pltpu.VMEM((2, cols, V * cols), BF16),
            pltpu.VMEM((cols, cells), F32),
            pltpu.SemaphoreType.DMA((2, n)),
            pltpu.SemaphoreType.DMA((2, n)),
            pltpu.SemaphoreType.DMA((2, ITERS, 2)),
            pltpu.SemaphoreType.DMA((2, ITERS, 2)),
            pltpu.SemaphoreType.DMA,
        ],
        compiler_params=pltpu.CompilerParams(
            collective_id=0, has_side_effects=True, vmem_limit_bytes=32 * 1024 * 1024
        ),
    )(
        camera_rows.reshape(V * zd * lr, n * cols),
        estimate.reshape(cells, cols),
        psf_bank.transpose(0, 2, 1, 3),
        psf_owner,
        view_mask.T,
    )
    return result.reshape(zd, rows, cols)


def solution(mesh):
    n = mesh.shape["plane"] * mesh.shape["brick"]

    def shards_of(camera_rows, estimate, psf_bank, psf_owner, view_mask):
        zd, rows, cols = estimate.shape
        lr = camera_rows.shape[2]
        small = (
            zd * rows == 256
            and cols == 128
            and psf_bank.shape[-1] == 2 * RADIUS + 1
            and lr * n == rows
            and zd % 8 == 0
            and zd * lr % 16 == 0
            and power_of_two(zd)
            and power_of_two(lr)
        )
        if not small:
            return shards(camera_rows, estimate, psf_bank, psf_owner, view_mask)
        dims = (n, mesh.shape["brick"], zd, rows, cols)
        return fused_shards(dims, camera_rows, estimate, psf_bank, psf_owner, view_mask)

    return jax.shard_map(
        shards_of,
        mesh=mesh,
        in_specs=(
            P(None, "slab", ("plane", "brick"), None),
            P("slab", None, ("plane", "brick")),
            P(("slab", "plane", "brick"), None, None, None),
            P("slab"),
            P("slab", None),
        ),
        out_specs=P("slab", None, ("plane", "brick")),
        check_vma=False,
    )
```

```python
import functools

import jax
import jax.numpy as jnp
from jax import lax
from jax.experimental import pallas as pl
from jax.experimental.pallas import tpu as pltpu
from jax.sharding import PartitionSpec as P

V = 4
RADIUS = 15
ITERS = 2
EDGE = 16


BACKGROUND = 0.1
HIGHEST = lax.Precision.HIGHEST
F32 = jnp.float32
BF16 = jnp.bfloat16
def padded_2(cells, sides, width):
    for axis, dim in sides:
        count = lax.axis_size(axis)
        ends = count - 1
        head = lax.slice_in_dim(cells, 0, width, axis=dim)
        tail = lax.slice_in_dim(cells, cells.shape[dim] - width, cells.shape[dim], axis=dim)
        cells = jnp.concatenate(
            [
                lax.ppermute(tail, axis, [(i, (i + 1) % count) for i in range(ends)]),
                cells,
                lax.ppermute(head, axis, [((i + 1) % count, i) for i in range(ends)]),
            ],
            axis=dim,
        )
    return cells


def banded(profiles, size_in, size_out, offset):
    tap_count = profiles.shape[-1]
    centre = tap_count // 2
    lag_index = (
        jnp.arange(size_in, dtype=jnp.int32)[:, None]
        - jnp.arange(size_out, dtype=jnp.int32)[None, :]
        - offset
        + centre
    )
    one_hot = (
        lag_index[:, :, None] == jnp.arange(tap_count, dtype=jnp.int32)[None, None, :]
    ).astype(jnp.float32)
    return jnp.einsum("ijt,vt->vij", one_hot, profiles, precision=HIGHEST)


def across_columns(volume, band_x):
    if volume.ndim == 3:
        return jnp.einsum("zyi,vij->vzyj", volume, band_x, precision=HIGHEST)
    return jnp.einsum("vzyi,vij->vzyj", volume, band_x, precision=HIGHEST)


def across_rows(volume, band_y):
    view_count, depth_count, row_count, col_count = volume.shape
    block_rows = band_y.shape[2]
    margin = (band_y.shape[1] - block_rows) // 2
    pieces = volume.reshape(view_count, depth_count, row_count // block_rows, block_rows, col_count)
    blanks = jnp.zeros((view_count, depth_count, 1, margin, col_count), jnp.float32)
    before = jnp.concatenate([blanks, pieces[:, :, :-1, block_rows - margin :, :]], axis=2)
    behind = jnp.concatenate([pieces[:, :, 1:, :margin, :], blanks], axis=2)
    windows = jnp.concatenate([before, pieces, behind], axis=3)
    result = jnp.einsum("vzqic,vij->vzqjc", windows, band_y, precision=HIGHEST)
    return result.reshape(view_count, depth_count, row_count, col_count)


def across_depth(volume, band_z):
    return jnp.einsum("vzyc,vzw->vwyc", volume, band_z, precision=HIGHEST)


def separable(volume, bands):
    return across_depth(across_rows(across_columns(volume, bands[0]), bands[1]), bands[2])


def shards(camera_rows, estimate, psf_bank, psf_owner, view_mask):
    regrouped = lax.all_to_all(
        camera_rows, ("plane", "brick"), split_axis=3, concat_axis=2, tiled=True
    )
    position = lax.axis_index(("plane", "brick"))
    brick_ids = jnp.arange(psf_owner.shape[0], dtype=jnp.int32)
    is_mine = brick_ids == position
    owner_id = jnp.sum(jnp.where(is_mine, psf_owner, 0))
    observed = jnp.sum(jnp.where(is_mine[:, None], view_mask, 0), axis=0) > 0
    fitted = lax.all_gather(psf_bank, ("plane", "brick"), axis=0, tiled=True)
    chosen = (brick_ids == owner_id).astype(jnp.float32)
    kernels = jnp.einsum("b,bvat->vat", chosen, fitted, precision=HIGHEST)
    kernels = kernels / jnp.sum(kernels, axis=-1, keepdims=True)
    flipped = kernels[:, :, ::-1]
    depth_size = estimate.shape[0]
    row_size = estimate.shape[1]
    col_size = estimate.shape[2]
    block_size = 128 if row_size % 128 == 0 else row_size

    def make_bands(profiles):
        return (
            banded(profiles[:, 2], col_size + 2 * RADIUS, col_size, RADIUS),
            banded(profiles[:, 1], block_size + 2 * RADIUS, block_size, RADIUS),
            banded(profiles[:, 0], depth_size, depth_size, 0),
        )

    blur_bands = make_bands(kernels)
    back_bands = make_bands(flipped)
    current = estimate
    for iteration in range(ITERS):
        padded = padded_2(current.astype(jnp.bfloat16), ((("plane", "brick"), 2),), RADIUS).astype(
            current.dtype
        )
        blurred = separable(padded, blur_bands)
        quotient = jnp.where(
            observed[:, None, None, None],
            regrouped.astype(jnp.float32) / (blurred + BACKGROUND),
            0.0,
        )
        quotient_wide = padded_2(
            quotient.astype(jnp.bfloat16), ((("plane", "brick"), 3),), RADIUS
        ).astype(quotient.dtype)
        corrected = separable(quotient_wide, back_bands)
        factor = jnp.sum(jnp.where(observed[:, None, None, None], corrected, 1.0), axis=0) / V
        current = current * factor
    return current


def split(a):
    hi = a.astype(BF16)
    return hi, (a - hi.astype(F32)).astype(BF16)


def dot(a, b, nt=False):
    dims = (((1,), (1 if nt else 0,)), ((), ()))
    return lax.dot_general(a, b, dims, preferred_element_type=F32)


def dot3(a, b, nt=False):
    return dot(a[0], b[0], nt) + (dot(a[0], b[1], nt) + dot(a[1], b[0], nt))


def dot2(a, b, nt=False):
    return dot(a, b[0], nt) + dot(a, b[1], nt)


def exact(a, b):
    return lax.dot_general(a, b, (((1,), (0,)), ((), ())), precision=HIGHEST, preferred_element_type=F32)


def fused(
    dims, cam, est, psf, owner, mask, out,
    taps, gath, camrecv, camt, xsend, xhalo, rsend, rhalo, kbh, kbl, abl, aback, xt,
    psf_sems, cam_sems, x_sems, r_sems, own_sem,
):
    n, brick, zd, rows, cols = dims
    lr = rows // n
    part = zd * lr
    cells = zd * rows
    taps_n = psf.shape[-1]
    me = lax.axis_index("plane") * brick + lax.axis_index("brick")

    def device(t):
        return {"plane": lax.div(t, brick), "brick": lax.rem(t, brick)}

    def peer(k):
        return lax.rem(me + k, n)

    barrier = pltpu.get_barrier_semaphore()
    for k in range(1, n):
        pl.semaphore_signal(barrier, inc=1, device_id=device(peer(k)), device_id_type=pl.DeviceIdType.MESH)

    has_left = me > 0
    has_right = me < n - 1
    zero_edge = jnp.zeros((EDGE, cells), BF16)

    @pl.when(me == 0)
    def _():
        for it in range(ITERS):
            xhalo[it, 0:EDGE, :] = zero_edge
            for v in range(V):
                rhalo[it, v, 0:EDGE, :] = zero_edge

    @pl.when(me == n - 1)
    def _():
        for it in range(ITERS):
            xhalo[it, EDGE:, :] = zero_edge
            for v in range(V):
                rhalo[it, v, EDGE:, :] = zero_edge

    def x_copy(it, side):
        rows_of = pl.ds(side * EDGE, EDGE)
        return pltpu.make_async_remote_copy(
            src_ref=xsend.at[it, rows_of], dst_ref=xhalo.at[it, rows_of],
            send_sem=x_sems.at[0, it, side], recv_sem=x_sems.at[1, it, side],
            device_id=device(lax.rem(me + n + 1 - 2 * side, n)), device_id_type=pl.DeviceIdType.MESH,
        )

    def r_copy(it, side):
        rows_of = pl.ds(side * EDGE, EDGE)
        return pltpu.make_async_remote_copy(
            src_ref=rsend.at[it, :, rows_of], dst_ref=rhalo.at[it, :, rows_of],
            send_sem=r_sems.at[0, it, side], recv_sem=r_sems.at[1, it, side],
            device_id=device(lax.rem(me + n + 1 - 2 * side, n)), device_id_type=pl.DeviceIdType.MESH,
        )

    def start(make, it):
        @pl.when(has_right)
        def _():
            make(it, 0).start()

        @pl.when(has_left)
        def _():
            make(it, 1).start()

    def arrive(make, it):
        @pl.when(has_left)
        def _():
            make(it, 0).wait_recv()

        @pl.when(has_right)
        def _():
            make(it, 1).wait_recv()

    def finish(make, it):
        @pl.when(has_right)
        def _():
            make(it, 0).wait_send()

        @pl.when(has_left)
        def _():
            make(it, 1).wait_send()

    def psf_copy(k):
        return pltpu.make_async_remote_copy(
            src_ref=psf.at[0], dst_ref=gath.at[me],
            send_sem=psf_sems.at[0, k], recv_sem=psf_sems.at[1, k],
            device_id=device(peer(k)), device_id_type=pl.DeviceIdType.MESH,
        )

    def cam_copy(k):
        return pltpu.make_async_remote_copy(
            src_ref=cam.at[:, pl.ds(pl.multiple_of(peer(k) * cols, cols), cols)], dst_ref=camrecv.at[me],
            send_sem=cam_sems.at[0, k], recv_sem=cam_sems.at[1, k],
            device_id=device(peer(k)), device_id_type=pl.DeviceIdType.MESH,
        )

    own = pltpu.make_async_copy(
        cam.at[:, pl.ds(pl.multiple_of(me * cols, cols), cols)], camrecv.at[me], own_sem
    )
    own.start()
    x0 = est[...].T
    xt[...] = x0
    xsend[0, 0:EDGE, :] = x0[cols - EDGE :, :].astype(BF16)
    xsend[0, EDGE:, :] = x0[:EDGE, :].astype(BF16)
    gath[me] = psf[0]

    pl.semaphore_wait(barrier, n - 1)
    ring_order = list(range(1, n))
    start(x_copy, 0)
    for k in ring_order:
        psf_copy(k).start()
    for k in ring_order:
        cam_copy(k).start()

    lane = lax.broadcasted_iota(jnp.int32, (128, cells), 1)
    line = lax.broadcasted_iota(jnp.int32, (128, cells), 0)
    y_of = lax.shift_right_logical(lane, part.bit_length() - 1) * lr + (lane & (lr - 1))
    z_of = lax.shift_right_logical(lane, lr.bit_length() - 1) & (zd - 1)
    pick_y = (y_of == line).astype(F32)
    pick_z = (z_of == line).astype(F32)
    flip = (
        lax.broadcasted_iota(jnp.int32, (128, 128), 0) + lax.broadcasted_iota(jnp.int32, (128, 128), 1)
        == taps_n - 1
    ).astype(F32)
    taps[...] = jnp.zeros_like(taps)

    for k in range(1, n):
        psf_copy(k).wait_recv()
    block = gath[owner[me]]
    for a in range(3):
        taps[a * V : (a + 1) * V, 0:taps_n] = block[a]
    kernels = taps[...]
    total = jnp.sum(kernels, axis=-1, keepdims=True)
    kernels = kernels / jnp.where(total > 0.0, total, 1.0)
    flipped = exact(kernels, flip)

    def toeplitz(row, height, width):
        if width > 128:
            row = jnp.concatenate([row, jnp.zeros((1, width - 128), F32)], axis=1)
        return pltpu.roll(
            jnp.broadcast_to(row, (height, width)), width - RADIUS, 1, stride=1, stride_axis=0
        )

    lines_y = jnp.concatenate([toeplitz(flipped[V + v : V + v + 1], rows, 128) for v in range(V)], axis=0)
    lines_z = jnp.concatenate([toeplitz(flipped[v : v + 1], zd, 128) for v in range(V)], axis=0)
    wide_y = exact(lines_y, pick_y)
    wide_z = exact(lines_z, pick_z)
    seen = [mask[v, me] > 0 for v in range(V)]
    back_edge = jnp.zeros((cols, 128), F32)
    for v in range(V):
        for z in range(zd):
            piece = wide_y[v * rows : (v + 1) * rows] * wide_z[v * zd + z : v * zd + z + 1]
            hi, lo = split(piece)
            kbh[v, z * rows : (z + 1) * rows, :] = hi
            kbl[v, z * rows : (z + 1) * rows, :] = lo
        band = toeplitz(kernels[2 * V + v : 2 * V + v + 1], cols, 2 * cols)
        hi, lo = split(band[:, :cols])
        abl[0, v] = hi
        abl[1, v] = lo
        hi, lo = split(pltpu.roll(band[:, cols:], EDGE, 1))
        abl[2, v] = hi
        abl[3, v] = lo
        band = jnp.where(seen[v], toeplitz(flipped[2 * V + v : 2 * V + v + 1], cols, 2 * cols), 0.0)
        hi, lo = split(band[:, :cols])
        aback[0, :, v * cols : (v + 1) * cols] = hi
        aback[1, :, v * cols : (v + 1) * cols] = lo
        back_edge = back_edge + pltpu.roll(band[:, cols:], (EDGE + 2 * EDGE * v) % 128, 1)
    back_edge = split(back_edge)
    unseen = functools.reduce(jnp.add, [jnp.where(s, 0.0, 1.0) for s in seen])

    for it in range(ITERS):
        x = split(xt[...])
        blurred = []
        for v in range(V):
            spread = split(dot3(x, (kbh[v], kbl[v])))
            blurred.append(dot3((abl[0, v], abl[1, v]), spread))
        arrive(x_copy, it)
        edge = xhalo[it]
        for v in range(V):
            spread = split(dot2(edge, (kbh[v], kbl[v])))
            blurred[v] = blurred[v] + dot3((abl[2, v, :, 0 : 2 * EDGE], abl[3, v, :, 0 : 2 * EDGE]), spread)
        if it == 0:
            for k in range(1, n):
                cam_copy(k).wait_recv()
            own.wait()
            for v in range(V):
                tile = camrecv[:, v * part : (v + 1) * part, :].reshape(cells, cols)
                camt[v] = tile.astype(F32).T
        ratios = []
        for v in range(V):
            ratio = jnp.where(seen[v], camt[v] / (blurred[v] + BACKGROUND), 0.0)
            rsend[it, v, 0:EDGE, :] = ratio[cols - EDGE :, :].astype(BF16)
            rsend[it, v, EDGE:, :] = ratio[:EDGE, :].astype(BF16)
            ratios.append(ratio)
        start(r_copy, it)
        spread = [split(dot3(split(ratios[v]), (kbh[v], kbl[v]), nt=True)) for v in range(V)]
        hi = jnp.concatenate([a for a, _ in spread], axis=0)
        lo = jnp.concatenate([b for _, b in spread], axis=0)
        total = dot3((aback[0], aback[1]), (hi, lo))
        arrive(r_copy, it)
        spread = [dot2(rhalo[it, v], (kbh[v], kbl[v]), nt=True) for v in range(V)]
        total = total + dot3(back_edge, split(jnp.concatenate(spread, axis=0)))
        fresh = xt[...] * ((total + unseen) * (1.0 / V))
        if it < ITERS - 1:
            xsend[it + 1, 0:EDGE, :] = fresh[cols - EDGE :, :].astype(BF16)
            xsend[it + 1, EDGE:, :] = fresh[:EDGE, :].astype(BF16)
            start(x_copy, it + 1)
            xt[...] = fresh
        else:
            out[...] = fresh.T

    for k in range(1, n):
        psf_copy(k).wait_send()
        cam_copy(k).wait_send()
    for it in range(ITERS):
        finish(x_copy, it)
        finish(r_copy, it)


def power_of_two(a):
    return a & (a - 1) == 0


def fused_shards(dims, camera_rows, estimate, psf_bank, psf_owner, view_mask):
    n, brick, zd, rows, cols = dims
    lr = rows // n
    cells = zd * rows
    vmem = pl.BlockSpec(memory_space=pltpu.VMEM)
    smem = pl.BlockSpec(memory_space=pltpu.SMEM)
    result = pl.pallas_call(
        functools.partial(fused, dims),
        out_shape=jax.ShapeDtypeStruct((cells, cols), F32),
        in_specs=[vmem, vmem, vmem, smem, smem],
        out_specs=vmem,
        scratch_shapes=[
            pltpu.VMEM((16, 128), F32),
            pltpu.VMEM((n, 3, V, psf_bank.shape[-1]), F32),
            pltpu.VMEM((n, V * zd * lr, cols), BF16),
            pltpu.VMEM((V, cols, cells), F32),
            pltpu.VMEM((ITERS, 2 * EDGE, cells), BF16),
            pltpu.VMEM((ITERS, 2 * EDGE, cells), BF16),
            pltpu.VMEM((ITERS, V, 2 * EDGE, cells), BF16),
            pltpu.VMEM((ITERS, V, 2 * EDGE, cells), BF16),
            pltpu.VMEM((V, cells, cells), BF16),
            pltpu.VMEM((V, cells, cells), BF16),
            pltpu.VMEM((4, V, cols, cols), BF16),
            pltpu.VMEM((2, cols, V * cols), BF16),
            pltpu.VMEM((cols, cells), F32),
            pltpu.SemaphoreType.DMA((2, n)),
            pltpu.SemaphoreType.DMA((2, n)),
            pltpu.SemaphoreType.DMA((2, ITERS, 2)),
            pltpu.SemaphoreType.DMA((2, ITERS, 2)),
            pltpu.SemaphoreType.DMA,
        ],
        compiler_params=pltpu.CompilerParams(
            collective_id=0, has_side_effects=True, vmem_limit_bytes=32 * 1024 * 1024
        ),
    )(
        camera_rows.reshape(V * zd * lr, n * cols),
        estimate.reshape(cells, cols),
        psf_bank.transpose(0, 2, 1, 3),
        psf_owner,
        view_mask.T,
    )
    return result.reshape(zd, rows, cols)


def solution(mesh):
    n = mesh.shape["plane"] * mesh.shape["brick"]

    def shards_of(camera_rows, estimate, psf_bank, psf_owner, view_mask):
        zd, rows, cols = estimate.shape
        lr = camera_rows.shape[2]
        small = (
            zd * rows == 256
            and cols == 128
            and psf_bank.shape[-1] == 2 * RADIUS + 1
            and lr * n == rows
            and zd % 8 == 0
            and zd * lr % 16 == 0
            and power_of_two(zd)
            and power_of_two(lr)
        )
        if not small:
            return shards(camera_rows, estimate, psf_bank, psf_owner, view_mask)
        dims = (n, mesh.shape["brick"], zd, rows, cols)
        return fused_shards(dims, camera_rows, estimate, psf_bank, psf_owner, view_mask)

    return jax.shard_map(
        shards_of,
        mesh=mesh,
        in_specs=(
            P(None, "slab", ("plane", "brick"), None),
            P("slab", None, ("plane", "brick")),
            P(("slab", "plane", "brick"), None, None, None),
            P("slab"),
            P("slab", None),
        ),
        out_specs=P("slab", None, ("plane", "brick")),
        check_vma=False,
    )
```
